512 devices in a mesh: strip: 8 (over x, core), dom: 64 (over y, z).
Axes of the slice: x: 4, y: 8, z: 8, core: 2. Of those that a mesh axis runs over, the one named last changes fastest.
Arguments:
- columns: bfloat16 [8, 196608, 128], P('strip', 'dom'), may hold values from -12 to 12
- regrid_weights: bfloat16 [8, 3072, 64, 128], P('strip', 'dom'), may hold values from 0.0019989014 to 0.059814453
- owner_table: int32 [8, 3072, 1], P('strip', 'dom'), may hold values from 0 to 63; in each aligned block of 48 rows (0 to 47, 48 to 95, ..., all dimensions but the last counted through in order) at most 2 rows name the same one
- grid_targets: int32 [8, 3072, 2], P('strip', 'dom'), may hold values from 0 to 15, all different within a row
- halo_send: int32 [8, 64, 2, 128], P('strip', 'dom'), may hold values from 0 to 3071
- halo_recv: int32 [8, 64, 2, 128], P('strip', 'dom'), may hold values from 0 to 3071
- coag: bfloat16 [128, 128], replicated, may hold values from -0.5 to 0.5
- settle_gain: float32 [128], replicated, may hold values from 2 to 20
Outputs:
- grid: bfloat16 [8, 65536, 128], P('strip', 'dom')
- columns_out: bfloat16 [8, 196608, 128], P('strip', 'dom')
The draws below stay inside these ranges and needn't reach their ends.
Inputs may be any that keep to these rules, and one draw needn't show every extreme that they name: `owner_table`: among the 48 column blocks of one partition at most 2 have the same owner, and some partition has exactly 2 with one owner. `grid_targets`: the two grid blocks of a column block differ.
All inputs are finite; a program needn't handle non-finite values.
Results may differ from the reference program's by a relative error of at most 0.0045.
Values may be sent and summed in bfloat16 or wider, within the bound.
A program may use at most 64 MiB of HBM per device.

```python
import math
import jax
import jax.numpy as jnp
import numpy as np
from jax import lax

CHAN = 128
BLK = 64
NB = 48
GB = 16
HALO = 128
CAP = 2
STRIPS = 8
PARTS_SIZE = 64
COLS_DEV = 3072
COLS = 196608
COLBLOCKS = 3072
GRIDCELLS = 65536
N_DOM = 64


def touch_ends(result, key, smallest, largest):
    place = [jax.random.randint(jax.random.fold_in(key, axis), (), 0, length) for axis, length in enumerate(result.shape)]
    longest = result.shape.index(max(result.shape))
    beside = place[:longest] + [(place[longest] + 1) % result.shape[longest]] + place[longest + 1:]
    return result.at[tuple(place)].set(smallest).at[tuple(beside)].set(largest)


def shard_levels(stream_key, dims, split, smallest, top_value):
    def one(position, shards_of):
        steps = jax.random.uniform(jax.random.fold_in(jax.random.fold_in(stream_key, 6), position), (shards_of,), jnp.float32, smallest / len(split), top_value / len(split))
        return jnp.repeat(jnp.exp(steps), dims[position] // shards_of).reshape((-1,) + (1,) * (len(dims) - position - 1))

    level = one(*split[0])
    for cut in split[1:]:
        level = level * one(*cut)
    return level


def picks_of(own_key, rows, amount, top, lift):
    sequence = jax.random.permutation(jax.random.fold_in(own_key, 1), amount)
    boost = sequence
    for power in range(3):
        boost = boost * boost // amount
    boost = boost * lift // amount
    lots = jax.random.randint(jax.random.fold_in(own_key, 2), (rows, amount), 0, 4096) + boost
    fixed_rows = jax.random.permutation(jax.random.fold_in(own_key, 3), rows)[jnp.arange(amount) % rows]
    lots = jnp.where(jnp.arange(rows)[:, None] == fixed_rows[None, :], 1 << 14, lots)
    priority = lots * amount + jnp.arange(amount)
    return lax.top_k(priority.astype(jnp.int32), top)[1].astype(jnp.int32)


def deal_out(rng, own, number, rows, number_of, top, limit, lean):
    order = jax.random.permutation(rng, number_of)
    heavy_load, common = shares(number_of, rows * top, limit, lean, True), shares(number_of, rows * top, limit, lean, False)
    places = jnp.arange(number_of)

    def named(tallies, rotation):
        used = int((tallies > 0).sum())
        fixed = max(1, used // 4)
        moved = fixed + (places - fixed + rotation * (used - fixed)) % max(1, number_of - fixed)
        return jnp.zeros((number_of,), jnp.int32).at[order[jnp.where(places < fixed, places, moved)]].set(jnp.asarray(tallies, jnp.int32))

    tallies = jnp.where(number % 4 == 0, named(heavy_load, number // 4), named(common, number - number // 4 - 1))
    mixed = jax.random.permutation(jax.random.fold_in(own, 3), number_of)
    giver, sink = mixed[0:number_of // 2 * 2:2], mixed[1:number_of // 2 * 2:2]
    margin = jnp.minimum(tallies[giver] - 1, limit - tallies[sink]) // 2
    margin = jnp.where((giver == order[0]) | (sink == order[0]) | (tallies[sink] == 0), 0, jnp.maximum(margin, 0))
    moved = jax.random.randint(jax.random.fold_in(own, 4), (number_of // 2,), 0, 1 << 20) % (margin + 1)
    tallies = tallies.at[giver].add(-moved).at[sink].add(moved)
    members = jnp.searchsorted(jnp.cumsum(tallies), jnp.arange(rows * top), side="right").astype(jnp.int32)
    table = members.reshape(top, rows).T
    table = table[jax.random.permutation(jax.random.fold_in(own, 1), rows)]
    rotation = jax.random.randint(jax.random.fold_in(own, 2), (rows, 1), 0, top)
    return jnp.take_along_axis(table, (jnp.arange(top)[None, :] + rotation) % top, axis=1)


def shares(number_of, total, most, lean, full):
    loads = [(1 << 20) // math.isqrt(standing ** lean) + 1 for standing in range(1, number_of + 1)]
    largest = most if full else min(most, max(-(-total // number_of), total * loads[0] // sum(loads)))
    least = 1 if total - largest >= number_of - 1 else 0
    given, rest = [largest] + [least] * (number_of - 1), total - largest - least * (number_of - 1)
    while rest > 0:
        candidates = [i for i in range(1, number_of) if given[i] < largest] or [i for i in range(1, number_of) if given[i] < most]
        mass, remaining = sum([loads[i] for i in candidates]), rest
        for i in candidates:
            addition = min(most - given[i], max(1, remaining * loads[i] // mass), rest)
            given[i] = given[i] + addition
            rest = rest - addition
    return np.array(given)


def gaussian(own_key, shape, width, bound, shards=(), kind=jnp.bfloat16):
    drawn = jax.random.normal(own_key, shape, jnp.float32) * width
    if len(shards) > 0:
        drawn = shard_levels(own_key, shape, shards, -0.22, 0.18) * drawn
    return jnp.clip(drawn, min=-bound, max=bound).astype(kind)


def setup_inputs(seed: int = 0) -> dict:
    keys = jax.random.split(jax.random.key(seed), 9)
    columns = gaussian(keys[0], (STRIPS, COLS, CHAN), 2.0, 12.0, ((0, 8), (1, 64)))
    regrid_weights = jnp.clip(jnp.exp(math.log(0.059814453) - 3.3986496 * jax.random.uniform(keys[1], (STRIPS, COLBLOCKS, BLK, 2 * BLK), jnp.float32) ** shard_levels(keys[1], (STRIPS, COLBLOCKS, BLK, 2 * BLK), ((0, 8), (1, 64)), -0.2, 0.2)), 0.0019989014, 0.059814453).astype(jnp.bfloat16)
    owner_table_keys = jax.random.split(jax.random.fold_in(keys[2], 1), STRIPS * COLBLOCKS // NB)
    owner_table_turns = jax.random.permutation(jax.random.fold_in(keys[2], 3), STRIPS * COLBLOCKS // NB)
    owner_table = jax.vmap(lambda own, number: deal_out(jax.random.fold_in(keys[2], 2), own, number, NB, N_DOM, 1, CAP, 2))(owner_table_keys, owner_table_turns).reshape((STRIPS, COLBLOCKS, 1))
    grid_targets = picks_of(keys[3], STRIPS * COLBLOCKS, GB, 2, 0).reshape((STRIPS, COLBLOCKS, 2))
    halo_send = touch_ends(jax.random.randint(keys[4], (STRIPS, PARTS_SIZE, 2, HALO), 0, COLS_DEV), jax.random.fold_in(keys[4], 1), 0, COLS_DEV - 1).astype(jnp.int32)
    halo_recv = touch_ends(jax.random.randint(keys[5], (STRIPS, PARTS_SIZE, 2, HALO), 0, COLS_DEV), jax.random.fold_in(keys[5], 1), 0, COLS_DEV - 1).astype(jnp.int32)
    coag = gaussian(keys[6], (CHAN, CHAN), CHAN ** -0.5, 0.5)
    settle_gain = jnp.clip(jnp.exp(jax.random.uniform(keys[7], (CHAN,), jnp.float32, math.log(2.0), math.log(20.0))), 2.0, 20.0)
    return dict(columns=columns, regrid_weights=regrid_weights, owner_table=owner_table, grid_targets=grid_targets, halo_send=halo_send, halo_recv=halo_recv, coag=coag, settle_gain=settle_gain)


def row_take(values, index_rows):
    return values[index_rows]


def row_add(values, index_rows, deltas):
    return values.at[index_rows].add(deltas)


def strip_regrid(packed):
    strip_cols, strip_weights, strip_owner, strip_targets, coag, settle_gain = packed
    blocks = strip_cols.reshape(COLBLOCKS, BLK, CHAN).astype(jnp.float32)
    weights = strip_weights.astype(jnp.float32)
    contrib = jnp.einsum("jcq,jch->jqh", weights, blocks)
    contrib = contrib.reshape(COLBLOCKS * 2, BLK, CHAN)
    grid_index = (strip_owner[:, 0:1] * GB + strip_targets).reshape(-1).astype(jnp.int32)
    numer = jnp.zeros((PARTS_SIZE * GB, BLK, CHAN), jnp.float32).at[grid_index].add(contrib)
    col_total = jnp.sum(weights, axis=1).reshape(COLBLOCKS * 2, BLK)
    denom = jnp.zeros((PARTS_SIZE * GB, BLK), jnp.float32).at[grid_index].add(col_total)
    grid = (numer / jnp.maximum(denom, 1.0)[:, :, None]).astype(jnp.bfloat16)
    mixed = jnp.dot(grid.reshape(-1, CHAN), coag, preferred_element_type=jnp.float32)
    flux = (settle_gain[None, :] * jnp.tanh(mixed)).astype(jnp.bfloat16)
    flux = flux.reshape(PARTS_SIZE * GB, BLK, CHAN)
    picked = flux[grid_index].reshape(COLBLOCKS, 2 * BLK, CHAN).astype(jnp.float32)
    returned = jnp.einsum("jcq,jqh->jch", weights, picked).astype(jnp.bfloat16)
    return grid.reshape(GRIDCELLS, CHAN), returned.reshape(COLS, CHAN)


def reference(columns, regrid_weights, owner_table, grid_targets, halo_send, halo_recv, coag, settle_gain):
    cols_float = columns.astype(jnp.float32)
    offsets = (jnp.arange(PARTS_SIZE, dtype=jnp.int32) * COLS_DEV)[None, :, None]
    send_upper = (halo_send[:, :, 0, :] + offsets).reshape(STRIPS, -1).astype(jnp.int32)
    send_lower = (halo_send[:, :, 1, :] + offsets).reshape(STRIPS, -1).astype(jnp.int32)
    recv_lower = (halo_recv[:, :, 0, :] + offsets).reshape(STRIPS, -1).astype(jnp.int32)
    recv_upper = (halo_recv[:, :, 1, :] + offsets).reshape(STRIPS, -1).astype(jnp.int32)
    take_rows = jax.vmap(row_take)
    up_values = take_rows(cols_float, send_upper)
    down_values = take_rows(cols_float, send_lower)
    from_lower = jnp.concatenate([jnp.zeros_like(up_values[:1]), up_values[:-1]], axis=0)
    from_upper = jnp.concatenate([down_values[1:], jnp.zeros_like(down_values[:1])], axis=0)
    strip_ids = jnp.arange(STRIPS, dtype=jnp.int32)[:, None, None]
    delta_lower = jnp.where(strip_ids > 0, from_lower - take_rows(cols_float, recv_lower), 0.0)
    delta_upper = jnp.where(strip_ids < STRIPS - 1, from_upper - take_rows(cols_float, recv_upper), 0.0)
    all_rows = jnp.concatenate([recv_lower, recv_upper], axis=1)
    all_deltas = 0.5 * jnp.concatenate([delta_lower, delta_upper], axis=1)
    relaxed = jax.vmap(row_add)(cols_float, all_rows, all_deltas)
    coag_all = jnp.broadcast_to(coag, (STRIPS,) + coag.shape)
    gain_all = jnp.broadcast_to(settle_gain, (STRIPS,) + settle_gain.shape)
    grid, returned = lax.map(strip_regrid, (columns, regrid_weights, owner_table, grid_targets, coag_all, gain_all))
    columns_out = (relaxed + returned.astype(jnp.float32)).astype(jnp.bfloat16)
    return grid, columns_out
```

```python
import functools
import jax
import jax.numpy as jnp
from jax import lax
from jax.experimental import pallas as pl
from jax.experimental.pallas import tpu as pltpu
from jax.sharding import PartitionSpec as P

MESH = pl.DeviceIdType.MESH
BF = jnp.bfloat16
F32 = jnp.float32
SIDE = 8
ORDER = (4, 3, 5, 2, 6, 1, 7)
PAIRS = ((0, 4), (3, 5), (2, 6), (1, 7))
CHUNK = 1040


def kernel(
    tab, slot_of, tsel, cols, wts, hsend_idx, hrecv_idx, coag, gain,
    grid_out, cols_out,
    abuf_s, abuf_r, tf, tr, wexp, acc, den, bsend, brecv, dtot, flux, dsend, drecv,
    relaxed, hrows, hsend, hrecv,
    a_s, a_r, b_s, b_r, c_s, c_r, d_s, d_r, h_s, h_r,
):
    strip = lax.axis_index("strip")
    dom = lax.axis_index("dom")
    strips = lax.axis_size("strip")
    y = dom // SIDE
    z = lax.rem(dom, SIDE)
    q = lax.rem(y + z, 2)

    def along(cls, dist):
        ny = lax.rem(y + (1 - cls) * dist + SIDE, SIDE)
        nz = lax.rem(z + cls * dist + SIDE, SIDE)
        return (strip, ny * SIDE + nz)

    barrier = pltpu.get_barrier_semaphore()
    for cls in range(2):
        for dist in range(1, SIDE):
            pl.semaphore_signal(barrier, inc=1, device_id=along(cls, dist), device_id_type=MESH)

    @pl.when(strip > 0)
    def _():
        pl.semaphore_signal(barrier, inc=1, device_id=(strip - 1, dom), device_id_type=MESH)

    @pl.when(strip < strips - 1)
    def _():
        pl.semaphore_signal(barrier, inc=1, device_id=(strip + 1, dom), device_id_type=MESH)

    def pack(dst, cls, dist):
        base = cls * 64 + dist * 8

        def one(s, carry):
            j = tab[base + s]
            dst[pl.ds(pl.multiple_of(s * 64, 64), 64), :] = cols[j]
            dst[pl.ds(pl.multiple_of(512 + s * 64, 64), 64), :] = wts[j]
            return carry

        lax.fori_loop(0, 8, one, 0)
        dst[pl.ds(1024, 16), :] = tsel[cls * 8 + dist]

    def pack_far(t, carry):
        cls, dist = t // 7, lax.rem(t, 7) + 1
        pack(abuf_s.at[cls, dist - 1], cls, dist)
        return carry

    lax.fori_loop(0, 14, pack_far, 0)

    neighbours = (strip > 0).astype(jnp.int32) + (strip < strips - 1).astype(jnp.int32)
    pl.semaphore_wait(barrier, 14 + neighbours)

    def a_copy(cls, dist):
        return pltpu.make_async_remote_copy(
            abuf_s.at[cls, dist - 1], abuf_r.at[cls, dist],
            a_s.at[cls, dist - 1], a_r.at[cls, dist - 1],
            device_id=along(cls, dist), device_id_type=MESH,
        )

    for dist in ORDER:
        for cls in range(2):
            a_copy(cls, dist).start()

    for cls in range(2):
        pack(abuf_r.at[cls, 0], cls, 0)

    idx = jnp.concatenate(
        [hsend_idx[...], hrecv_idx[...], jnp.zeros((4, 128), jnp.int32)], axis=0
    ).astype(F32)
    idx_t = idx.T
    hrows[...] = jnp.zeros_like(hrows)

    def gather(kc, carry):
        block = cols[pl.ds(kc * 4, 4)].reshape(256, 128)
        lane = lax.broadcasted_iota(jnp.int32, (128, 256), 1) + kc * 256
        lane = lane.astype(F32)
        for l in range(4):
            hot = jnp.where(idx_t[:, l : l + 1] == lane, 1.0, 0.0).astype(BF)
            hrows[l] += jnp.dot(hot, block, preferred_element_type=F32)
        return carry

    lax.fori_loop(0, 12, gather, 0)
    hsend[...] = hrows[pl.ds(0, 2)].astype(BF)

    def h_copy(way):
        step = 1 - 2 * way
        return pltpu.make_async_remote_copy(
            hsend.at[way], hrecv.at[way], h_s.at[way], h_r.at[way],
            device_id=(strip + step, dom), device_id_type=MESH,
        )

    @pl.when(strip < strips - 1)
    def _():
        h_copy(0).start()

    @pl.when(strip > 0)
    def _():
        h_copy(1).start()

    par = jnp.where(lax.broadcasted_iota(jnp.int32, (1, 128), 1) >= 64, 1.0, 0.0)
    twice = 2.0 * lax.broadcasted_iota(jnp.int32, (8, 128), 0).astype(F32)
    den[...] = jnp.zeros_like(den)

    def expand(cls, i, o, d, row0):
        for rr in range(2):
            w = abuf_r[cls, d, pl.ds(pl.multiple_of(512 + i * 128 + rr * 64, 64), 64), :]
            u = tf[cls, d, pl.ds(2 * i + rr, 1), :] - par
            v = tr[cls, d, pl.ds(2 * i + rr, 1), :] - par
            wf = w.astype(F32)
            wrf = pltpu.roll(wf, 64, 1)
            wr = wrf.astype(BF)
            total = jnp.sum(wf, axis=0, keepdims=True)
            turned = jnp.sum(wrf, axis=0, keepdims=True)
            den[o] += jnp.where(u == twice, total, 0.0) + jnp.where(v == twice, turned, 0.0)
            ub = jnp.broadcast_to(u, (16, 128))
            vb = jnp.broadcast_to(v, (16, 128))
            for m in range(8):
                a = jnp.where(ub == 2.0 * m, 1.0, 0.0).astype(BF)
                b = jnp.where(vb == 2.0 * m, 1.0, 0.0).astype(BF)
                a4 = jnp.concatenate([a] * 4, axis=0)
                b4 = jnp.concatenate([b] * 4, axis=0)
                wexp[o, pl.ds(row0 + rr * 64, 64), pl.ds(m * 128, 128)] = w * a4 + wr * b4

    def tile_step(pos, cls, i):
        o = cls * 4 + i
        d1, d2 = PAIRS[pos]
        expand(cls, i, o, d1, pos * 256)
        expand(cls, i, o, d2, pos * 256 + 128)
        rows = pl.ds(pl.multiple_of(i * 128, 128), 128)
        xt = jnp.concatenate([abuf_r[cls, d1, rows, :].T, abuf_r[cls, d2, rows, :].T], axis=1)
        for mm in range(4):
            lanes = pl.ds(mm * 256, 256)
            part = jnp.dot(
                xt, wexp[o, pl.ds(pos * 256, 256), lanes], preferred_element_type=F32
            )
            if pos == 0:
                acc[o, :, lanes] = part
            else:
                acc[o, :, lanes] += part

    def arrive(pos, cls):
        for d in PAIRS[pos]:
            if d > 0:
                a_copy(cls, d).wait_recv()
            t = abuf_r[cls, d, pl.ds(1024, 16), :].astype(F32)[0:8]
            tf[cls, d] = t
            tr[cls, d] = pltpu.roll(t, 64, 1)

    for pos in range(3):

        def half(cls, carry, pos=pos):
            arrive(pos, cls)

            def tile(i, c):
                tile_step(pos, cls, i)
                return c

            return lax.fori_loop(0, 4, tile, carry)

        lax.fori_loop(0, 2, half, 0)

    @pl.when(strip > 0)
    def _():
        h_copy(0).wait_recv()

    @pl.when(strip == 0)
    def _():
        hrecv[0] = jnp.zeros((128, 128), BF)

    @pl.when(strip < strips - 1)
    def _():
        h_copy(1).wait_recv()

    @pl.when(strip == strips - 1)
    def _():
        hrecv[1] = jnp.zeros((128, 128), BF)

    keep = (
        jnp.where(strip > 0, 0.5, 0.0).astype(F32),
        jnp.where(strip < strips - 1, 0.5, 0.0).astype(F32),
    )
    for way in range(2):
        delta = keep[way] * (hrecv[way].astype(F32) - hrows[2 + way])
        high = delta.astype(BF)
        hrows[2 + way] = delta
        hsplit = (high, (delta - high.astype(F32)).astype(BF))
        if way == 0:
            split0 = hsplit
        else:
            split1 = hsplit
    highs = jnp.concatenate([split0[0], split1[0]], axis=0)
    lows = jnp.concatenate([split0[1], split1[1]], axis=0)

    def relax(kc, carry):
        row = (lax.broadcasted_iota(jnp.int32, (256, 128), 0) + kc * 256)
        hot = jnp.concatenate(
            [
                jnp.where(row == hrecv_idx[pl.ds(0, 1), :], 1.0, 0.0).astype(BF),
                jnp.where(row == hrecv_idx[pl.ds(1, 1), :], 1.0, 0.0).astype(BF),
            ],
            axis=1,
        )
        moved = jnp.dot(hot, highs, preferred_element_type=F32)
        moved += jnp.dot(hot, lows, preferred_element_type=F32)
        block = cols[pl.ds(kc * 4, 4)].reshape(256, 128).astype(F32)
        relaxed[pl.ds(kc * 4, 4)] = (block + moved).reshape(4, 64, 128)
        return carry

    lax.fori_loop(0, 12, relax, 0)

    def b_parts(cls, a):
        dist = 2 * a + (1 - cls) * q + cls * (1 - q)
        coord = (1 - cls) * z + cls * y
        i = lax.rem(coord + dist, SIDE) // 2
        return dist, i

    def b_copy(cls, a):
        dist, i = b_parts(cls, a)
        slot = jnp.maximum(dist, 1) - 1
        return pltpu.make_async_remote_copy(
            bsend.at[cls * 4 + i], brecv.at[slot], b_s.at[cls, a], b_r.at[slot],
            device_id=along(1 - cls, dist), device_id_type=MESH,
        )

    for cls in range(2):
        arrive(3, cls)

    def last(t, carry):
        cls, a = lax.rem(t, 2), t // 2
        dist, i = b_parts(cls, a)
        tile_step(3, cls, i)
        o = cls * 4 + i

        @pl.when(dist > 0)
        def _():
            for m in range(8):
                bsend[o, pl.ds(m * 128, 128), :] = acc[o, :, pl.ds(m * 128, 128)].astype(BF)
            dd = den[o]
            high = dd.astype(BF)
            low = (dd - high.astype(F32)).astype(BF)
            bsend[o, pl.ds(1024, 16), :] = jnp.concatenate([high, low], axis=0)
            b_copy(cls, a).start()

        return carry

    lax.fori_loop(0, 8, last, 0)

    own = q * 4 + ((1 - q) * z + q * y) // 2
    dsum = den[own]
    for d in range(7):
        pltpu.make_async_remote_copy(
            bsend.at[0], brecv.at[d], b_s.at[0, 0], b_r.at[d],
            device_id=along(0, 1), device_id_type=MESH,
        ).wait_recv()
        two = brecv[d, pl.ds(1024, 16), :].astype(F32)
        dsum = dsum + two[0:8] + two[8:16]
    dtot[...] = jnp.maximum(dsum, 1.0)

    def finish(m, carry):
        rows = pl.ds(pl.multiple_of(m * 128, 128), 128)
        num = acc[own, :, rows]
        for d in range(7):
            num += brecv[d, rows, :].astype(F32)
        g = (num / dtot[pl.ds(m, 1), :]).T.astype(BF)
        grid_out[rows, :] = g
        mixed = jnp.dot(g, coag[...], preferred_element_type=F32)
        flux[own, rows, :] = (gain[...] * jnp.tanh(mixed)).astype(BF)
        return carry

    lax.fori_loop(0, 8, finish, 0)

    def c_copy(dist):
        return pltpu.make_async_remote_copy(
            flux.at[own], flux.at[own], c_s.at[dist - 1], c_r.at[own],
            device_id=along(1 - q, dist), device_id_type=MESH,
        )

    for dist in ORDER:
        c_copy(dist).start()

    def d_copy(cls, i, dist):
        pair = pl.ds(i * 2, 2)
        o = cls * 4 + i
        return pltpu.make_async_remote_copy(
            dsend.at[cls, dist - 1, pair], drecv.at[pl.ds(cls * 64 + dist * 8 + i * 2, 2)],
            d_s.at[o, dist - 1], d_r.at[o, dist - 1],
            device_id=along(cls, SIDE - dist), device_id_type=MESH,
        )

    def back(t, carry):
        o = lax.rem(own + t, 8)
        cls, i = o // 4, lax.rem(o, 4)

        @pl.when(t > 0)
        def _():
            pltpu.make_async_remote_copy(
                flux.at[o], flux.at[o], c_s.at[0], c_r.at[o],
                device_id=along(0, 1), device_id_type=MESH,
            ).wait_recv()

        tile = flux[o]
        for pos in range(4):
            r = jnp.dot(
                wexp[o, pl.ds(pos * 256, 256), :], tile, preferred_element_type=F32
            ).astype(BF)
            for h in range(2):
                d = PAIRS[pos][h]
                two = r[h * 128 : h * 128 + 128].reshape(2, 64, 128)
                if d == 0:
                    drecv[pl.ds(cls * 64 + i * 2, 2)] = two
                else:
                    dsend[cls, d - 1, pl.ds(i * 2, 2)] = two
        for dist in ORDER:
            d_copy(cls, i, dist).start()
        return carry

    lax.fori_loop(0, 8, back, 0)

    def gather_back(o, carry):
        for dist in range(1, SIDE):
            d_copy(o // 4, lax.rem(o, 4), dist).wait_recv()
        return carry

    lax.fori_loop(0, 8, gather_back, 0)

    def final(j, carry):
        cols_out[j] = (relaxed[j] + drecv[slot_of[j]].astype(F32)).astype(BF)
        return carry

    lax.fori_loop(0, 48, final, 0)

    for dist in range(1, SIDE):
        for cls in range(2):
            a_copy(cls, dist).wait_send()
        c_copy(dist).wait_send()

    @pl.when(strip < strips - 1)
    def _():
        h_copy(0).wait_send()

    @pl.when(strip > 0)
    def _():
        h_copy(1).wait_send()

    def b_sent(t, carry):
        cls, a = lax.rem(t, 2), t // 2

        @pl.when(b_parts(cls, a)[0] > 0)
        def _():
            b_copy(cls, a).wait_send()

        return carry

    lax.fori_loop(0, 8, b_sent, 0)

    def d_sent(o, carry):
        for dist in range(1, SIDE):
            d_copy(o // 4, lax.rem(o, 4), dist).wait_send()
        return carry

    lax.fori_loop(0, 8, d_sent, 0)


def shards(
    columns, regrid_weights, owner_table, grid_targets, halo_send, halo_recv, coag, settle_gain
):
    nblocks, blk, chans = regrid_weights.shape[1], regrid_weights.shape[2], columns.shape[2]
    dom = lax.axis_index("dom")
    y, z = dom // SIDE, lax.rem(dom, SIDE)
    owners = owner_table[0, :, 0]
    ids = jnp.arange(nblocks, dtype=jnp.int32)
    rank = jnp.sum(
        ((owners[:, None] == owners[None, :]) & (ids[None, :] < ids[:, None])).astype(jnp.int32),
        axis=1,
    )
    oy, oz = owners // SIDE, lax.rem(owners, SIDE)
    cls = lax.rem(oy + oz, 2)
    dist = jnp.where(cls == 0, oy - y + SIDE, oz - z + SIDE) % SIDE
    slot_of = cls * 64 + dist * 8 + jnp.where(cls == 0, oz, oy) // 2 * 2 + rank
    hot = slot_of[None, :] == jnp.arange(128, dtype=jnp.int32)[:, None]
    tab = jnp.max(jnp.where(hot, ids[None, :], 0), axis=1)
    t01 = jnp.max(jnp.where(hot[:, None, :], grid_targets[0].T[None], -1), axis=2)
    tsel = jnp.repeat(t01, 64, axis=1).astype(BF).reshape(16, 8, 128)
    tsel = jnp.concatenate([tsel, tsel], axis=1)

    vmem = pl.BlockSpec(memory_space=pltpu.VMEM)
    smem = pl.BlockSpec(memory_space=pltpu.SMEM)
    dma = pltpu.SemaphoreType.DMA
    grid, out = pl.pallas_call(
        kernel,
        out_shape=(
            jax.ShapeDtypeStruct((1024, chans), BF),
            jax.ShapeDtypeStruct((nblocks, blk, chans), BF),
        ),
        in_specs=[smem, smem] + [vmem] * 7,
        out_specs=(vmem, vmem),
        scratch_shapes=[
            pltpu.VMEM((2, 7, CHUNK, 128), BF),
            pltpu.VMEM((2, 8, CHUNK, 128), BF),
            pltpu.VMEM((2, 8, 8, 128), F32),
            pltpu.VMEM((2, 8, 8, 128), F32),
            pltpu.VMEM((8, 1024, 1024), BF),
            pltpu.VMEM((8, 128, 1024), F32),
            pltpu.VMEM((8, 8, 128), F32),
            pltpu.VMEM((8, CHUNK, 128), BF),
            pltpu.VMEM((7, CHUNK, 128), BF),
            pltpu.VMEM((8, 128), F32),
            pltpu.VMEM((8, 1024, 128), BF),
            pltpu.VMEM((2, 7, 8, 64, 128), BF),
            pltpu.VMEM((128, 64, 128), BF),
            pltpu.VMEM((48, 64, 128), F32),
            pltpu.VMEM((4, 128, 128), F32),
            pltpu.VMEM((2, 128, 128), BF),
            pltpu.VMEM((2, 128, 128), BF),
            dma((2, 7)), dma((2, 7)),
            dma((2, 4)), dma((7,)),
            dma((7,)), dma((8,)),
            dma((8, 7)), dma((8, 7)),
            dma((2,)), dma((2,)),
        ],
        compiler_params=pltpu.CompilerParams(
            collective_id=0, has_side_effects=True, vmem_limit_bytes=56 * 2**20
        ),
    )(
        tab, slot_of, tsel,
        columns[0].reshape(nblocks, blk, chans), regrid_weights[0],
        halo_send[0, 0], halo_recv[0, 0], coag, settle_gain[None, :],
    )
    return grid[None], out.reshape(1, nblocks * blk, chans)


def solution(mesh):
    placed = (
        P("strip", "dom", None),
        P("strip", "dom", None, None),
        P("strip", "dom", None),
        P("strip", "dom", None),
        P("strip", "dom", None, None),
        P("strip", "dom", None, None),
        P(),
        P(),
    )
    return jax.shard_map(
        shards,
        mesh=mesh,
        in_specs=placed,
        out_specs=(P("strip", "dom", None), P("strip", "dom", None)),
        check_vma=False,
    )
```

```python
import functools
import jax
import jax.numpy as jnp
from jax import lax
from jax.experimental import pallas as pl
from jax.experimental.pallas import tpu as pltpu
from jax.sharding import PartitionSpec as P

MESH = pl.DeviceIdType.MESH
BF = jnp.bfloat16
F32 = jnp.float32
SIDE = 8
ORDER = (4, 3, 5, 2, 6, 1, 7)
PAIRS = ((0, 4), (3, 5), (2, 6), (1, 7))
CHUNK = 1040


def kernel(
    tab, slot_of, tsel, cols, wts, hsend_idx, hrecv_idx, coag, gain,
    grid_out, cols_out,
    abuf_s, abuf_r, tf, tr, wexp, acc, den, bsend, brecv, dtot, flux, dsend, drecv,
    relaxed, hrows, hsend, hrecv,
    a_s, a_r, b_s, b_r, c_s, c_r, d_s, d_r, h_s, h_r,
):
    strip = lax.axis_index("strip")
    dom = lax.axis_index("dom")
    strips = lax.axis_size("strip")
    y = dom // SIDE
    z = lax.rem(dom, SIDE)
    q = lax.rem(y + z, 2)

    def along(cls, dist):
        ny = lax.rem(y + (1 - cls) * dist + SIDE, SIDE)
        nz = lax.rem(z + cls * dist + SIDE, SIDE)
        return (strip, ny * SIDE + nz)

    barrier = pltpu.get_barrier_semaphore()
    for cls in range(2):
        for dist in range(1, SIDE):
            pl.semaphore_signal(barrier, inc=1, device_id=along(cls, dist), device_id_type=MESH)

    @pl.when(strip > 0)
    def _():
        pl.semaphore_signal(barrier, inc=1, device_id=(strip - 1, dom), device_id_type=MESH)

    @pl.when(strip < strips - 1)
    def _():
        pl.semaphore_signal(barrier, inc=1, device_id=(strip + 1, dom), device_id_type=MESH)

    def pack(dst, cls, dist):
        base = cls * 64 + dist * 8

        def one(s, carry):
            j = tab[base + s]
            dst[pl.ds(pl.multiple_of(s * 64, 64), 64), :] = cols[j]
            dst[pl.ds(pl.multiple_of(512 + s * 64, 64), 64), :] = wts[j]
            return carry

        lax.fori_loop(0, 8, one, 0)
        dst[pl.ds(1024, 16), :] = tsel[cls * 8 + dist]

    def pack_far(t, carry):
        cls, dist = t // 7, lax.rem(t, 7) + 1
        pack(abuf_s.at[cls, dist - 1], cls, dist)
        return carry

    lax.fori_loop(0, 14, pack_far, 0)

    neighbours = (strip > 0).astype(jnp.int32) + (strip < strips - 1).astype(jnp.int32)
    pl.semaphore_wait(barrier, 14 + neighbours)

    def a_copy(cls, dist):
        return pltpu.make_async_remote_copy(
            abuf_s.at[cls, dist - 1], abuf_r.at[cls, dist],
            a_s.at[cls, dist - 1], a_r.at[cls, dist - 1],
            device_id=along(cls, dist), device_id_type=MESH,
        )

    for dist in ORDER:
        for cls in range(2):
            a_copy(cls, dist).start()

    for cls in range(2):
        pack(abuf_r.at[cls, 0], cls, 0)

    idx = jnp.concatenate(
        [hsend_idx[...], hrecv_idx[...], jnp.zeros((4, 128), jnp.int32)], axis=0
    ).astype(F32)
    idx_t = idx.T
    hrows[...] = jnp.zeros_like(hrows)

    def gather(kc, carry):
        block = cols[pl.ds(kc * 4, 4)].reshape(256, 128)
        lane = lax.broadcasted_iota(jnp.int32, (128, 256), 1) + kc * 256
        lane = lane.astype(F32)
        for l in range(4):
            hot = jnp.where(idx_t[:, l : l + 1] == lane, 1.0, 0.0).astype(BF)
            hrows[l] += jnp.dot(hot, block, preferred_element_type=F32)
        return carry

    lax.fori_loop(0, 12, gather, 0)
    hsend[...] = hrows[pl.ds(0, 2)].astype(BF)

    def h_copy(way):
        step = 1 - 2 * way
        return pltpu.make_async_remote_copy(
            hsend.at[way], hrecv.at[way], h_s.at[way], h_r.at[way],
            device_id=(strip + step, dom), device_id_type=MESH,
        )

    @pl.when(strip < strips - 1)
    def _():
        h_copy(0).start()

    @pl.when(strip > 0)
    def _():
        h_copy(1).start()

    par = jnp.where(lax.broadcasted_iota(jnp.int32, (1, 128), 1) >= 64, 1.0, 0.0)
    twice = 2.0 * lax.broadcasted_iota(jnp.int32, (8, 128), 0).astype(F32)
    den[...] = jnp.zeros_like(den)

    def expand(cls, i, o, d, row0):
        for rr in range(2):
            w = abuf_r[cls, d, pl.ds(pl.multiple_of(512 + i * 128 + rr * 64, 64), 64), :]
            u = tf[cls, d, pl.ds(2 * i + rr, 1), :] - par
            v = tr[cls, d, pl.ds(2 * i + rr, 1), :] - par
            wf = w.astype(F32)
            wrf = pltpu.roll(wf, 64, 1)
            wr = wrf.astype(BF)
            total = jnp.sum(wf, axis=0, keepdims=True)
            turned = jnp.sum(wrf, axis=0, keepdims=True)
            den[o] += jnp.where(u == twice, total, 0.0) + jnp.where(v == twice, turned, 0.0)
            ub = jnp.broadcast_to(u, (16, 128))
            vb = jnp.broadcast_to(v, (16, 128))
            for m in range(8):
                a = jnp.where(ub == 2.0 * m, 1.0, 0.0).astype(BF)
                b = jnp.where(vb == 2.0 * m, 1.0, 0.0).astype(BF)
                a4 = jnp.concatenate([a] * 4, axis=0)
                b4 = jnp.concatenate([b] * 4, axis=0)
                wexp[o, pl.ds(row0 + rr * 64, 64), pl.ds(m * 128, 128)] = w * a4 + wr * b4

    def tile_step(pos, cls, i):
        o = cls * 4 + i
        d1, d2 = PAIRS[pos]
        expand(cls, i, o, d1, pos * 256)
        expand(cls, i, o, d2, pos * 256 + 128)
        rows = pl.ds(pl.multiple_of(i * 128, 128), 128)
        xt = jnp.concatenate([abuf_r[cls, d1, rows, :].T, abuf_r[cls, d2, rows, :].T], axis=1)
        for mm in range(4):
            part = jnp.dot(
                xt, wexp[o, pl.ds(pos * 256, 256), pl.ds(mm * 256, 256)], preferred_element_type=F32
            )
            for h in range(2):
                piece = part[:, h * 128 : h * 128 + 128]
                if pos == 0:
                    acc[o, 2 * mm + h] = piece
                else:
                    acc[o, 2 * mm + h] += piece

    def arrive(pos, cls):
        for d in PAIRS[pos]:
            if d > 0:
                a_copy(cls, d).wait_recv()
            t = abuf_r[cls, d, pl.ds(1024, 16), :].astype(F32)[0:8]
            tf[cls, d] = t
            tr[cls, d] = pltpu.roll(t, 64, 1)

    for pos in range(3):

        def half(cls, carry, pos=pos):
            arrive(pos, cls)

            def tile(i, c):
                tile_step(pos, cls, i)
                return c

            return lax.fori_loop(0, 4, tile, carry)

        lax.fori_loop(0, 2, half, 0)

    @pl.when(strip > 0)
    def _():
        h_copy(0).wait_recv()

    @pl.when(strip == 0)
    def _():
        hrecv[0] = jnp.zeros((128, 128), BF)

    @pl.when(strip < strips - 1)
    def _():
        h_copy(1).wait_recv()

    @pl.when(strip == strips - 1)
    def _():
        hrecv[1] = jnp.zeros((128, 128), BF)

    keep = (
        jnp.where(strip > 0, 0.5, 0.0).astype(F32),
        jnp.where(strip < strips - 1, 0.5, 0.0).astype(F32),
    )
    for way in range(2):
        delta = keep[way] * (hrecv[way].astype(F32) - hrows[2 + way])
        high = delta.astype(BF)
        hrows[2 + way] = delta
        hsplit = (high, (delta - high.astype(F32)).astype(BF))
        if way == 0:
            split0 = hsplit
        else:
            split1 = hsplit
    highs = jnp.concatenate([split0[0], split1[0]], axis=0)
    lows = jnp.concatenate([split0[1], split1[1]], axis=0)

    def relax(kc, carry):
        row = (lax.broadcasted_iota(jnp.int32, (256, 128), 0) + kc * 256)
        hot = jnp.concatenate(
            [
                jnp.where(row == hrecv_idx[pl.ds(0, 1), :], 1.0, 0.0).astype(BF),
                jnp.where(row == hrecv_idx[pl.ds(1, 1), :], 1.0, 0.0).astype(BF),
            ],
            axis=1,
        )
        moved = jnp.dot(hot, highs, preferred_element_type=F32)
        moved += jnp.dot(hot, lows, preferred_element_type=F32)
        block = cols[pl.ds(kc * 4, 4)].reshape(256, 128).astype(F32)
        relaxed[pl.ds(kc * 4, 4)] = (block + moved).reshape(4, 64, 128)
        return carry

    lax.fori_loop(0, 12, relax, 0)

    hcoord = (1 - q) * z + q * y
    ccoord = (1 - q) * y + q * z

    def tile_at(home, t):
        coord = hcoord if home else ccoord
        return (q if home else 1 - q) * 4 + lax.rem(coord + t + SIDE, SIDE) // 2

    def next_to(home, way):
        return along(1 - q if home else q, 1 - 2 * way)

    def whole(t, way):
        return (0, 4) if t < 4 else ((0, 2), (2, 4))[way]

    def b_copy(t, way, ck):
        return pltpu.make_async_remote_copy(
            bsend.at[t - 1, way, ck], brecv.at[t - 1, way, ck],
            b_s.at[t - 1, way, ck], b_r.at[t - 1, way, ck],
            device_id=next_to(t % 2 == 0, way), device_id_type=MESH,
        )

    def b_total(t, way, ck, o):
        num = acc[o, pl.ds(ck * 2, 2)].reshape(256, 128)
        dd = den[o]
        if t < 4:
            wide = brecv[t, way, ck].astype(F32)
            num = num + wide[0:256]
            dd = dd + wide[256:264] + wide[264:272]
        return num, dd

    def b_hop(t, way):
        o = tile_at(t % 2 == 0, t * (1 - 2 * way))

        def send(ck, carry, further):
            if further:
                b_copy(t + 1, way, ck).wait_recv()
            num, dd = b_total(t if further else 4, way, ck, o)
            high = dd.astype(BF)
            low = (dd - high.astype(F32)).astype(BF)
            bsend[t - 1, way, ck, pl.ds(0, 256), :] = num.astype(BF)
            bsend[t - 1, way, ck, pl.ds(256, 16), :] = jnp.concatenate([high, low], axis=0)
            b_copy(t, way, ck).start()
            return carry

        lo, hi = whole(t, way)
        flo, fhi = whole(t + 1, way) if t < 4 else (0, 0)
        if lo < flo:
            lax.fori_loop(lo, flo, functools.partial(send, further=False), 0)
        if max(lo, fhi) < hi:
            lax.fori_loop(max(lo, fhi), hi, functools.partial(send, further=False), 0)
        if flo < fhi:
            lax.fori_loop(flo, fhi, functools.partial(send, further=True), 0)

    for cls in range(2):
        arrive(3, cls)

    def last(o):
        tile_step(3, o // 4, lax.rem(o, 4))

    last(tile_at(True, 4))
    for way in range(2):
        b_hop(4, way)
    for t in (3, 2, 1):
        for way in range(2):
            last(tile_at(t % 2 == 0, t * (1 - 2 * way)))
        for way in range(2):
            b_hop(t, way)
    own = tile_at(True, 0)
    last(own)

    def c_copy(t, way, ck):
        o = tile_at(t % 2 == 1, -(t - 1) * (1 - 2 * way))
        rows = pl.ds(pl.multiple_of(ck * 256, 256), 256)
        return pltpu.make_async_remote_copy(
            flux.at[o, rows], flux.at[o, rows], c_s.at[t - 1, way, ck], c_r.at[o, ck],
            device_id=next_to(t % 2 == 1, way), device_id_type=MESH,
        )

    def c_arrive(o, ck):
        rows = pl.ds(pl.multiple_of(ck * 256, 256), 256)
        pltpu.make_async_remote_copy(
            flux.at[o, rows], flux.at[o, rows], c_s.at[0, 0, 0], c_r.at[o, ck],
            device_id=next_to(True, 0), device_id_type=MESH,
        ).wait_recv()

    def finish(ck, carry):
        for way in range(2):
            b_copy(1, way, ck).wait_recv()
        wide = brecv[0, 0, ck].astype(F32) + brecv[0, 1, ck].astype(F32)
        dtot[...] = jnp.maximum(den[own] + wide[256:264] + wide[264:272], 1.0)
        for h in range(2):
            num = acc[own, ck * 2 + h] + wide[h * 128 : h * 128 + 128]
            rows = pl.ds(pl.multiple_of(ck * 256 + h * 128, 128), 128)
            g = (num / dtot[pl.ds(ck * 2 + h, 1), :]).T.astype(BF)
            grid_out[rows, :] = g
            mixed = jnp.dot(g, coag[...], preferred_element_type=F32)
            flux[own, rows, :] = (gain[...] * jnp.tanh(mixed)).astype(BF)
        for way in range(2):
            c_copy(1, way, ck).start()
        return carry

    lax.fori_loop(0, 4, finish, 0)

    def d_copy(cls, i, dist):
        pair = pl.ds(i * 2, 2)
        o = cls * 4 + i
        return pltpu.make_async_remote_copy(
            dsend.at[cls, dist - 1, pair], drecv.at[pl.ds(cls * 64 + dist * 8 + i * 2, 2)],
            d_s.at[o, dist - 1], d_r.at[o, dist - 1],
            device_id=along(cls, SIDE - dist), device_id_type=MESH,
        )

    def back(o):
        cls, i = o // 4, lax.rem(o, 4)
        tile = flux[o]
        for pos in range(4):
            r = jnp.dot(
                wexp[o, pl.ds(pos * 256, 256), :], tile, preferred_element_type=F32
            ).astype(BF)
            for h in range(2):
                d = PAIRS[pos][h]
                two = r[h * 128 : h * 128 + 128].reshape(2, 64, 128)
                if d == 0:
                    drecv[pl.ds(cls * 64 + i * 2, 2)] = two
                else:
                    dsend[cls, d - 1, pl.ds(i * 2, 2)] = two
        for dist in ORDER:
            d_copy(cls, i, dist).start()

    back(own)
    for t in (1, 2, 3):
        tiles = [tile_at(t % 2 == 0, -t * (1 - 2 * way)) for way in range(2)]

        def relay(ck, carry, t=t, tiles=tiles):
            for way in range(2):
                c_arrive(tiles[way], ck)
                lo, hi = whole(t + 1, way)

                @pl.when((ck >= lo) & (ck < hi))
                def _():
                    c_copy(t + 1, way, ck).start()

            return carry

        lax.fori_loop(0, 4, relay, 0)
        for way in range(2):
            back(tiles[way])
    far = tile_at(True, 4)
    for ck in range(4):
        c_arrive(far, ck)
    back(far)

    def gather_back(o, carry):
        for dist in range(1, SIDE):
            d_copy(o // 4, lax.rem(o, 4), dist).wait_recv()
        return carry

    lax.fori_loop(0, 8, gather_back, 0)

    def final(j, carry):
        cols_out[j] = (relaxed[j] + drecv[slot_of[j]].astype(F32)).astype(BF)
        return carry

    lax.fori_loop(0, 48, final, 0)

    for dist in range(1, SIDE):
        for cls in range(2):
            a_copy(cls, dist).wait_send()

    @pl.when(strip < strips - 1)
    def _():
        h_copy(0).wait_send()

    @pl.when(strip > 0)
    def _():
        h_copy(1).wait_send()

    for t in range(1, 5):
        for way in range(2):
            for ck in range(*whole(t, way)):
                b_copy(t, way, ck).wait_send()
                c_copy(t, way, ck).wait_send()

    def d_sent(o, carry):
        for dist in range(1, SIDE):
            d_copy(o // 4, lax.rem(o, 4), dist).wait_send()
        return carry

    lax.fori_loop(0, 8, d_sent, 0)


def shards(
    columns, regrid_weights, owner_table, grid_targets, halo_send, halo_recv, coag, settle_gain
):
    nblocks, blk, chans = regrid_weights.shape[1], regrid_weights.shape[2], columns.shape[2]
    dom = lax.axis_index("dom")
    y, z = dom // SIDE, lax.rem(dom, SIDE)
    owners = owner_table[0, :, 0]
    ids = jnp.arange(nblocks, dtype=jnp.int32)
    rank = jnp.sum(
        ((owners[:, None] == owners[None, :]) & (ids[None, :] < ids[:, None])).astype(jnp.int32),
        axis=1,
    )
    oy, oz = owners // SIDE, lax.rem(owners, SIDE)
    cls = lax.rem(oy + oz, 2)
    dist = jnp.where(cls == 0, oy - y + SIDE, oz - z + SIDE) % SIDE
    slot_of = cls * 64 + dist * 8 + jnp.where(cls == 0, oz, oy) // 2 * 2 + rank
    hot = slot_of[None, :] == jnp.arange(128, dtype=jnp.int32)[:, None]
    tab = jnp.max(jnp.where(hot, ids[None, :], 0), axis=1)
    t01 = jnp.max(jnp.where(hot[:, None, :], grid_targets[0].T[None], -1), axis=2)
    tsel = jnp.repeat(t01, 64, axis=1).astype(BF).reshape(16, 8, 128)
    tsel = jnp.concatenate([tsel, tsel], axis=1)

    vmem = pl.BlockSpec(memory_space=pltpu.VMEM)
    smem = pl.BlockSpec(memory_space=pltpu.SMEM)
    dma = pltpu.SemaphoreType.DMA
    grid, out = pl.pallas_call(
        kernel,
        out_shape=(
            jax.ShapeDtypeStruct((1024, chans), BF),
            jax.ShapeDtypeStruct((nblocks, blk, chans), BF),
        ),
        in_specs=[smem, smem] + [vmem] * 7,
        out_specs=(vmem, vmem),
        scratch_shapes=[
            pltpu.VMEM((2, 7, CHUNK, 128), BF),
            pltpu.VMEM((2, 8, CHUNK, 128), BF),
            pltpu.VMEM((2, 8, 8, 128), F32),
            pltpu.VMEM((2, 8, 8, 128), F32),
            pltpu.VMEM((8, 1024, 1024), BF),
            pltpu.VMEM((8, 8, 128, 128), F32),
            pltpu.VMEM((8, 8, 128), F32),
            pltpu.VMEM((4, 2, 4, 272, 128), BF),
            pltpu.VMEM((4, 2, 4, 272, 128), BF),
            pltpu.VMEM((8, 128), F32),
            pltpu.VMEM((8, 1024, 128), BF),
            pltpu.VMEM((2, 7, 8, 64, 128), BF),
            pltpu.VMEM((128, 64, 128), BF),
            pltpu.VMEM((48, 64, 128), F32),
            pltpu.VMEM((4, 128, 128), F32),
            pltpu.VMEM((2, 128, 128), BF),
            pltpu.VMEM((2, 128, 128), BF),
            dma((2, 7)), dma((2, 7)),
            dma((4, 2, 4)), dma((4, 2, 4)),
            dma((4, 2, 4)), dma((8, 4)),
            dma((8, 7)), dma((8, 7)),
            dma((2,)), dma((2,)),
        ],
        compiler_params=pltpu.CompilerParams(
            collective_id=0, has_side_effects=True, vmem_limit_bytes=56 * 2**20
        ),
    )(
        tab, slot_of, tsel,
        columns[0].reshape(nblocks, blk, chans), regrid_weights[0],
        halo_send[0, 0], halo_recv[0, 0], coag, settle_gain[None, :],
    )
    return grid[None], out.reshape(1, nblocks * blk, chans)


def solution(mesh):
    placed = (
        P("strip", "dom", None),
        P("strip", "dom", None, None),
        P("strip", "dom", None),
        P("strip", "dom", None),
        P("strip", "dom", None, None),
        P("strip", "dom", None, None),
        P(),
        P(),
    )
    return jax.shard_map(
        shards,
        mesh=mesh,
        in_specs=placed,
        out_specs=(P("strip", "dom", None), P("strip", "dom", None)),
        check_vma=False,
    )
```

```python
import jax
import jax.numpy as jnp
from jax import lax
from jax.experimental import pallas as pl
from jax.experimental.pallas import tpu as pltpu
from jax.sharding import PartitionSpec as P

MESH = pl.DeviceIdType.MESH
BF = jnp.bfloat16
F32 = jnp.float32
SIDE = 8
CHUNKS = 8
ORDER = (4, 3, 5, 2, 6, 1, 7)
PARTS = 4


def kernel(
    tab, slot_of, tsel, cols, wts, hsend_idx, hrecv_idx, coag, gain,
    grid_out, cols_out,
    abuf_s, abuf_r, trecv, tf, tr, xt, wexp, acc, den, bsend, brecv, dtot, flux, dsend, drecv,
    relaxed, hrows, hsend, hrecv,
    t_s, t_r, a_s, a_r, b_s, b_r, c_s, c_r, d_s, d_r, h_s, h_r,
):
    strip = lax.axis_index("strip")
    dom = lax.axis_index("dom")
    strips = lax.axis_size("strip")
    y = dom // SIDE
    z = lax.rem(dom, SIDE)
    q = lax.rem(y + z, 2)

    def along(cls, dist):
        ny = lax.rem(y + (1 - cls) * dist + SIDE, SIDE)
        nz = lax.rem(z + cls * dist + SIDE, SIDE)
        return (strip, ny * SIDE + nz)

    barrier = pltpu.get_barrier_semaphore()
    for cls in range(2):
        for dist in range(1, SIDE):
            pl.semaphore_signal(barrier, inc=1, device_id=along(cls, dist), device_id_type=MESH)

    @pl.when(strip > 0)
    def _():
        pl.semaphore_signal(barrier, inc=1, device_id=(strip - 1, dom), device_id_type=MESH)

    @pl.when(strip < strips - 1)
    def _():
        pl.semaphore_signal(barrier, inc=1, device_id=(strip + 1, dom), device_id_type=MESH)

    def pack(dst, cls, dist):
        base = cls * 64 + dist * 8

        def one(k, carry):
            for r in range(2):
                j = tab[base + k * 2 + r]
                dst[k, pl.ds(r * 64, 64), :] = cols[j]
                dst[k, pl.ds(128 + r * 64, 64), :] = wts[j]
            return carry

        lax.fori_loop(0, PARTS, one, 0)

    def pack_far(t, carry):
        cls, dist = t // 7, lax.rem(t, 7) + 1
        pack(abuf_s.at[cls, dist - 1], cls, dist)
        return carry

    lax.fori_loop(0, 14, pack_far, 0)

    neighbours = (strip > 0).astype(jnp.int32) + (strip < strips - 1).astype(jnp.int32)
    pl.semaphore_wait(barrier, 14 + neighbours)

    def t_copy(cls, dist):
        return pltpu.make_async_remote_copy(
            tsel.at[cls * 8 + dist], trecv.at[cls, dist],
            t_s.at[cls, dist - 1], t_r.at[cls, dist - 1],
            device_id=along(cls, dist), device_id_type=MESH,
        )

    def a_copy(cls, dist, k):
        return pltpu.make_async_remote_copy(
            abuf_s.at[cls, dist - 1, k], abuf_r.at[cls, dist, k],
            a_s.at[cls, dist - 1, k], a_r.at[cls, dist - 1, k],
            device_id=along(cls, dist), device_id_type=MESH,
        )

    for dist in ORDER:
        for cls in range(2):
            t_copy(cls, dist).start()

    def a_start(k, carry):
        for dist in ORDER:
            for cls in range(2):
                a_copy(cls, dist, k).start()
        return carry

    lax.fori_loop(0, 2, a_start, 0)

    for cls in range(2):
        pack(abuf_r.at[cls, 0], cls, 0)
        trecv[cls, 0] = tsel[cls * 8]

    idx = jnp.concatenate(
        [hsend_idx[...], hrecv_idx[...], jnp.zeros((4, 128), jnp.int32)], axis=0
    ).astype(F32)
    idx_t = idx.T
    hrows[...] = jnp.zeros_like(hrows)

    def gather(kc, carry):
        block = cols[pl.ds(kc * 4, 4)].reshape(256, 128)
        lane = lax.broadcasted_iota(jnp.int32, (128, 256), 1) + kc * 256
        lane = lane.astype(F32)
        for l in range(4):
            hot = jnp.where(idx_t[:, l : l + 1] == lane, 1.0, 0.0).astype(BF)
            hrows[l] += jnp.dot(hot, block, preferred_element_type=F32)
        return carry

    lax.fori_loop(0, 12, gather, 0)
    hsend[...] = hrows[pl.ds(0, 2)].astype(BF)

    def h_copy(way):
        step = 1 - 2 * way
        return pltpu.make_async_remote_copy(
            hsend.at[way], hrecv.at[way], h_s.at[way], h_r.at[way],
            device_id=(strip + step, dom), device_id_type=MESH,
        )

    @pl.when(strip < strips - 1)
    def _():
        h_copy(0).start()

    @pl.when(strip > 0)
    def _():
        h_copy(1).start()

    par = jnp.where(lax.broadcasted_iota(jnp.int32, (1, 128), 1) >= 64, 1.0, 0.0)
    twice = 2.0 * lax.broadcasted_iota(jnp.int32, (8, 128), 0).astype(F32)
    den[...] = jnp.zeros_like(den)

    def expand(cls, o, d, k):
        for rr in range(2):
            w = abuf_r[cls, d, k, pl.ds(128 + rr * 64, 64), :]
            u = tf[cls, d, pl.ds(2 * k + rr, 1), :] - par
            v = tr[cls, d, pl.ds(2 * k + rr, 1), :] - par
            wf = w.astype(F32)
            wrf = pltpu.roll(wf, 64, 1)
            wr = wrf.astype(BF)
            total = jnp.sum(wf, axis=0, keepdims=True)
            turned = jnp.sum(wrf, axis=0, keepdims=True)
            den[o] += jnp.where(u == twice, total, 0.0) + jnp.where(v == twice, turned, 0.0)
            ub = jnp.broadcast_to(u, (16, 128))
            vb = jnp.broadcast_to(v, (16, 128))
            rows = pl.ds(pl.multiple_of(d * 128 + rr * 64, 64), 64)
            for m in range(8):
                a = jnp.where(ub == 2.0 * m, 1.0, 0.0).astype(BF)
                b = jnp.where(vb == 2.0 * m, 1.0, 0.0).astype(BF)
                a4 = jnp.concatenate([a] * 4, axis=0)
                b4 = jnp.concatenate([b] * 4, axis=0)
                wexp[o, rows, pl.ds(m * 128, 128)] = w * a4 + wr * b4

    hcoord = (1 - q) * z + q * y
    ccoord = (1 - q) * y + q * z

    def tile_at(home, t):
        coord = hcoord if home else ccoord
        return (q if home else 1 - q) * 4 + lax.rem(coord + t + SIDE, SIDE) // 2

    def next_to(home, way):
        return along(1 - q if home else q, 1 - 2 * way)

    def add_up(t):
        home = t % 2 == 0
        k = 3 - t if t < 4 else t - 4
        cls = q if home else 1 - q
        o = tile_at(home, t)

        def source(e, carry):
            far = jnp.where(lax.rem(e, 2) == 0, 4 - e // 2, 4 + e // 2)
            d = jnp.where(e == 0, 0, far)

            @pl.when(e > 0)
            def _():
                a_copy(cls, jnp.maximum(d, 1), k).wait_recv()

            expand(cls, o, d, k)
            lanes = pl.ds(pl.multiple_of(d * 128, 128), 128)
            xt[:, lanes] = abuf_r[cls, d, k, pl.ds(0, 128), :].T
            return carry

        lax.fori_loop(0, 8, source, 0)
        for mm in range(4):
            part = jnp.dot(xt[...], wexp[o, :, pl.ds(mm * 256, 256)], preferred_element_type=F32)
            for h in range(2):
                acc[o, 2 * mm + h] = part[:, h * 128 : h * 128 + 128]

    def see(e, carry):
        cls, d = e // 8, lax.rem(e, 8)

        @pl.when(d > 0)
        def _():
            t_copy(cls, jnp.maximum(d, 1)).wait_recv()

        t = trecv[cls, d].astype(F32)[0:8]
        tf[cls, d] = t
        tr[cls, d] = pltpu.roll(t, 64, 1)
        return carry

    lax.fori_loop(0, 16, see, 0)

    def whole(t, way):
        half = CHUNKS // 2
        return (0, CHUNKS) if t < 4 else ((0, half), (half, CHUNKS))[way]

    def b_copy(t, way, ck):
        return pltpu.make_async_remote_copy(
            bsend.at[t - 1, way, ck], brecv.at[t - 1, way, ck],
            b_s.at[t - 1, way, ck], b_r.at[t - 1, way, ck],
            device_id=next_to(t % 2 == 0, way), device_id_type=MESH,
        )

    def b_total(t, way, ck, o):
        num = acc[o, ck]
        dd = den[o]
        if t < 4:
            wide = brecv[t, way, ck].astype(F32)
            num = num + wide[0:128]
            dd = dd + wide[128:136] + wide[136:144]
        return num, dd

    def b_hop(t, ways):
        def send(ck, way):
            o = tile_at(t % 2 == 0, t * (1 - 2 * way))
            if t == 4:
                ship(t, way, ck, *b_total(4, way, ck, o))
            elif t == 3:
                lo, hi = whole(4, way)
                further = (ck >= lo) & (ck < hi)

                @pl.when(further)
                def _():
                    b_copy(4, way, ck).wait_recv()
                    ship(t, way, ck, *b_total(t, way, ck, o))

                @pl.when(jnp.logical_not(further))
                def _():
                    ship(t, way, ck, *b_total(4, way, ck, o))
            else:
                b_copy(t + 1, way, ck).wait_recv()
                ship(t, way, ck, *b_total(t, way, ck, o))

        def both(ck, carry):
            for way in ways:
                send(ck, way)
            return carry

        if t == 4:
            half = CHUNKS // 2

            def four(ck, carry):
                send(ck, 0)
                send(ck + half, 1)
                return carry

            lax.fori_loop(0, half, four, 0)
        else:
            lax.fori_loop(0, CHUNKS, both, 0)

    def ship(t, way, ck, num, dd):
        high = dd.astype(BF)
        low = (dd - high.astype(F32)).astype(BF)
        bsend[t - 1, way, ck, pl.ds(0, 128), :] = num.astype(BF)
        bsend[t - 1, way, ck, pl.ds(128, 16), :] = jnp.concatenate([high, low], axis=0)
        b_copy(t, way, ck).start()

    add_up(4)
    b_hop(4, (0, 1))
    a_start(2, 0)
    add_up(3)
    add_up(5)
    b_hop(3, (0, 1))
    a_start(3, 0)

    @pl.when(strip > 0)
    def _():
        h_copy(0).wait_recv()

    @pl.when(strip == 0)
    def _():
        hrecv[0] = jnp.zeros((128, 128), BF)

    @pl.when(strip < strips - 1)
    def _():
        h_copy(1).wait_recv()

    @pl.when(strip == strips - 1)
    def _():
        hrecv[1] = jnp.zeros((128, 128), BF)

    keep = (
        jnp.where(strip > 0, 0.5, 0.0).astype(F32),
        jnp.where(strip < strips - 1, 0.5, 0.0).astype(F32),
    )
    for way in range(2):
        delta = keep[way] * (hrecv[way].astype(F32) - hrows[2 + way])
        high = delta.astype(BF)
        hrows[2 + way] = delta
        hsplit = (high, (delta - high.astype(F32)).astype(BF))
        if way == 0:
            split0 = hsplit
        else:
            split1 = hsplit
    highs = jnp.concatenate([split0[0], split1[0]], axis=0)
    lows = jnp.concatenate([split0[1], split1[1]], axis=0)

    def relax(kc, carry):
        row = (lax.broadcasted_iota(jnp.int32, (256, 128), 0) + kc * 256)
        hot = jnp.concatenate(
            [
                jnp.where(row == hrecv_idx[pl.ds(0, 1), :], 1.0, 0.0).astype(BF),
                jnp.where(row == hrecv_idx[pl.ds(1, 1), :], 1.0, 0.0).astype(BF),
            ],
            axis=1,
        )
        moved = jnp.dot(hot, highs, preferred_element_type=F32)
        moved += jnp.dot(hot, lows, preferred_element_type=F32)
        block = cols[pl.ds(kc * 4, 4)].reshape(256, 128).astype(F32)
        relaxed[pl.ds(kc * 4, 4)] = (block + moved).reshape(4, 64, 128)
        return carry

    lax.fori_loop(0, 12, relax, 0)

    add_up(2)
    add_up(6)
    b_hop(2, (0, 1))
    add_up(1)
    add_up(7)
    b_hop(1, (0, 1))
    own = tile_at(True, 0)
    add_up(0)

    def c_copy(t, way, ck):
        o = tile_at(t % 2 == 1, -(t - 1) * (1 - 2 * way))
        rows = pl.ds(pl.multiple_of(ck * 128, 128), 128)
        return pltpu.make_async_remote_copy(
            flux.at[o, rows], flux.at[o, rows], c_s.at[t - 1, way, ck], c_r.at[o, ck],
            device_id=next_to(t % 2 == 1, way), device_id_type=MESH,
        )

    def c_arrive(o, ck):
        rows = pl.ds(pl.multiple_of(ck * 128, 128), 128)
        pltpu.make_async_remote_copy(
            flux.at[o, rows], flux.at[o, rows], c_s.at[0, 0, 0], c_r.at[o, ck],
            device_id=next_to(True, 0), device_id_type=MESH,
        ).wait_recv()

    def finish(ck, carry):
        for way in range(2):
            b_copy(1, way, ck).wait_recv()
        wide = brecv[0, 0, ck].astype(F32) + brecv[0, 1, ck].astype(F32)
        dtot[...] = jnp.maximum(den[own] + wide[128:136] + wide[136:144], 1.0)
        rows = pl.ds(pl.multiple_of(ck * 128, 128), 128)
        g = ((acc[own, ck] + wide[0:128]) / dtot[pl.ds(ck, 1), :]).T.astype(BF)
        grid_out[rows, :] = g
        mixed = jnp.dot(g, coag[...], preferred_element_type=F32)
        flux[own, rows, :] = (gain[...] * jnp.tanh(mixed)).astype(BF)
        for way in range(2):
            c_copy(1, way, ck).start()
        return carry

    lax.fori_loop(0, CHUNKS, finish, 0)

    def d_copy(cls, k, dist):
        pair = pl.ds(k * 2, 2)
        o = cls * 4 + k
        return pltpu.make_async_remote_copy(
            dsend.at[cls, dist - 1, pair], drecv.at[pl.ds(cls * 64 + dist * 8 + k * 2, 2)],
            d_s.at[o, dist - 1], d_r.at[o, dist - 1],
            device_id=along(cls, SIDE - dist), device_id_type=MESH,
        )

    def back(o, k):
        cls = o // 4
        tile = flux[o]
        for pos in range(4):
            r = jnp.dot(
                wexp[o, pl.ds(pos * 256, 256), :], tile, preferred_element_type=F32
            ).astype(BF)
            for h in range(2):
                d = pos * 2 + h
                two = r[h * 128 : h * 128 + 128].reshape(2, 64, 128)
                if d == 0:
                    drecv[pl.ds(cls * 64 + k * 2, 2)] = two
                else:
                    dsend[cls, d - 1, pl.ds(k * 2, 2)] = two
        for dist in ORDER:
            d_copy(cls, k, dist).start()

    waiting = [(own, 3)]
    for t in (1, 2, 3):
        tiles = [tile_at(t % 2 == 0, -t * (1 - 2 * way)) for way in range(2)]

        def relay(ck, carry, t=t, tiles=tiles):
            for way in range(2):
                c_arrive(tiles[way], ck)
                lo, hi = whole(t + 1, way)

                @pl.when((ck >= lo) & (ck < hi))
                def _():
                    c_copy(t + 1, way, ck).start()

            return carry

        lax.fori_loop(0, CHUNKS, relay, 0)
        for pair in waiting:
            back(*pair)
        waiting = [(tiles[way], 4 - t - way) for way in range(2)]
    for pair in waiting:
        back(*pair)
    far = tile_at(True, 4)
    for ck in range(CHUNKS):
        c_arrive(far, ck)
    back(far, 0)

    def gather_back(o, carry):
        for dist in range(1, SIDE):
            d_copy(o // 4, lax.rem(o, 4), dist).wait_recv()
        return carry

    lax.fori_loop(0, 8, gather_back, 0)

    def final(j, carry):
        cols_out[j] = (relaxed[j] + drecv[slot_of[j]].astype(F32)).astype(BF)
        return carry

    lax.fori_loop(0, 48, final, 0)

    def a_sent(k, carry):
        for dist in range(1, SIDE):
            for cls in range(2):
                a_copy(cls, dist, k).wait_send()
        return carry

    lax.fori_loop(0, PARTS, a_sent, 0)
    for dist in range(1, SIDE):
        for cls in range(2):
            t_copy(cls, dist).wait_send()

    @pl.when(strip < strips - 1)
    def _():
        h_copy(0).wait_send()

    @pl.when(strip > 0)
    def _():
        h_copy(1).wait_send()

    for t in range(1, 5):
        for way in range(2):
            for ck in range(*whole(t, way)):
                b_copy(t, way, ck).wait_send()
                c_copy(t, way, ck).wait_send()

    def d_sent(o, carry):
        for dist in range(1, SIDE):
            d_copy(o // 4, lax.rem(o, 4), dist).wait_send()
        return carry

    lax.fori_loop(0, 8, d_sent, 0)


def shards(
    columns, regrid_weights, owner_table, grid_targets, halo_send, halo_recv, coag, settle_gain
):
    nblocks, blk, chans = regrid_weights.shape[1], regrid_weights.shape[2], columns.shape[2]
    dom = lax.axis_index("dom")
    y, z = dom // SIDE, lax.rem(dom, SIDE)
    owners = owner_table[0, :, 0]
    ids = jnp.arange(nblocks, dtype=jnp.int32)
    rank = jnp.sum(
        ((owners[:, None] == owners[None, :]) & (ids[None, :] < ids[:, None])).astype(jnp.int32),
        axis=1,
    )
    oy, oz = owners // SIDE, lax.rem(owners, SIDE)
    cls = lax.rem(oy + oz, 2)
    dist = jnp.where(cls == 0, oy - y + SIDE, oz - z + SIDE) % SIDE
    away = jnp.where(cls == 0, oz - z + SIDE, oy - y + SIDE) % SIDE
    slot_of = cls * 64 + dist * 8 + jnp.where(away < 4, 3 - away, away - 4) * 2 + rank
    hot = slot_of[None, :] == jnp.arange(128, dtype=jnp.int32)[:, None]
    tab = jnp.max(jnp.where(hot, ids[None, :], 0), axis=1)
    t01 = jnp.max(jnp.where(hot[:, None, :], grid_targets[0].T[None], -1), axis=2)
    tsel = jnp.repeat(t01, 64, axis=1).astype(BF).reshape(16, 8, 128)
    tsel = jnp.concatenate([tsel, tsel], axis=1)

    vmem = pl.BlockSpec(memory_space=pltpu.VMEM)
    smem = pl.BlockSpec(memory_space=pltpu.SMEM)
    dma = pltpu.SemaphoreType.DMA
    grid, out = pl.pallas_call(
        kernel,
        out_shape=(
            jax.ShapeDtypeStruct((1024, chans), BF),
            jax.ShapeDtypeStruct((nblocks, blk, chans), BF),
        ),
        in_specs=[smem, smem] + [vmem] * 7,
        out_specs=(vmem, vmem),
        scratch_shapes=[
            pltpu.VMEM((2, 7, PARTS, 256, 128), BF),
            pltpu.VMEM((2, 8, PARTS, 256, 128), BF),
            pltpu.VMEM((2, 8, 16, 128), BF),
            pltpu.VMEM((2, 8, 8, 128), F32),
            pltpu.VMEM((2, 8, 8, 128), F32),
            pltpu.VMEM((128, 1024), BF),
            pltpu.VMEM((8, 1024, 1024), BF),
            pltpu.VMEM((8, 8, 128, 128), F32),
            pltpu.VMEM((8, 8, 128), F32),
            pltpu.VMEM((4, 2, CHUNKS, 144, 128), BF),
            pltpu.VMEM((4, 2, CHUNKS, 144, 128), BF),
            pltpu.VMEM((8, 128), F32),
            pltpu.VMEM((8, 1024, 128), BF),
            pltpu.VMEM((2, 7, 8, 64, 128), BF),
            pltpu.VMEM((128, 64, 128), BF),
            pltpu.VMEM((48, 64, 128), F32),
            pltpu.VMEM((4, 128, 128), F32),
            pltpu.VMEM((2, 128, 128), BF),
            pltpu.VMEM((2, 128, 128), BF),
            dma((2, 7)), dma((2, 7)),
            dma((2, 7, PARTS)), dma((2, 7, PARTS)),
            dma((4, 2, CHUNKS)), dma((4, 2, CHUNKS)),
            dma((4, 2, CHUNKS)), dma((8, CHUNKS)),
            dma((8, 7)), dma((8, 7)),
            dma((2,)), dma((2,)),
        ],
        compiler_params=pltpu.CompilerParams(
            collective_id=0, has_side_effects=True, vmem_limit_bytes=56 * 2**20
        ),
    )(
        tab, slot_of, tsel,
        columns[0].reshape(nblocks, blk, chans), regrid_weights[0],
        halo_send[0, 0], halo_recv[0, 0], coag, settle_gain[None, :],
    )
    return grid[None], out.reshape(1, nblocks * blk, chans)


def solution(mesh):
    placed = (
        P("strip", "dom", None),
        P("strip", "dom", None, None),
        P("strip", "dom", None),
        P("strip", "dom", None),
        P("strip", "dom", None, None),
        P("strip", "dom", None, None),
        P(),
        P(),
    )
    return jax.shard_map(
        shards,
        mesh=mesh,
        in_specs=placed,
        out_specs=(P("strip", "dom", None), P("strip", "dom", None)),
        check_vma=False,
    )
```

```python
import jax
import jax.numpy as jnp
from jax import lax
from jax.experimental import pallas as pl
from jax.experimental.pallas import tpu as pltpu
from jax.sharding import PartitionSpec as P

MESH = pl.DeviceIdType.MESH
BF = jnp.bfloat16
F32 = jnp.float32
SIDE = 8
CHUNKS = 8
ORDER = (4, 3, 5, 2, 6, 1, 7)
PARTS = 4


def kernel(
    tab, slot_of, tsel, cols, wts, hsend_idx, hrecv_idx, coag, gain,
    grid_out, cols_out,
    abuf_s, abuf_r, trecv, tf, tr, xt, wexp, acc, den, bsend, brecv, dtot, flux, dsend, drecv,
    relaxed, hrows, hsend, hrecv,
    t_s, t_r, a_s, a_r, b_s, b_r, c_s, c_r, d_s, d_r, h_s, h_r,
):
    strip = lax.axis_index("strip")
    dom = lax.axis_index("dom")
    strips = lax.axis_size("strip")
    y = dom // SIDE
    z = lax.rem(dom, SIDE)
    q = lax.rem(y + z, 2)

    def along(cls, dist):
        ny = lax.rem(y + (1 - cls) * dist + SIDE, SIDE)
        nz = lax.rem(z + cls * dist + SIDE, SIDE)
        return (strip, ny * SIDE + nz)

    barrier = pltpu.get_barrier_semaphore()
    for cls in range(2):
        for dist in range(1, SIDE):
            pl.semaphore_signal(barrier, inc=1, device_id=along(cls, dist), device_id_type=MESH)

    @pl.when(strip > 0)
    def _():
        pl.semaphore_signal(barrier, inc=1, device_id=(strip - 1, dom), device_id_type=MESH)

    @pl.when(strip < strips - 1)
    def _():
        pl.semaphore_signal(barrier, inc=1, device_id=(strip + 1, dom), device_id_type=MESH)

    def pack(dst, cls, dist):
        base = cls * 64 + dist * 8

        def one(k, carry):
            for r in range(2):
                j = tab[base + k * 2 + r]
                dst[k, pl.ds(r * 64, 64), :] = cols[j]
                dst[k, pl.ds(128 + r * 64, 64), :] = wts[j]
            return carry

        lax.fori_loop(0, PARTS, one, 0)

    def pack_far(t, carry):
        cls, dist = t // 7, lax.rem(t, 7) + 1
        pack(abuf_s.at[cls, dist - 1], cls, dist)
        return carry

    lax.fori_loop(0, 14, pack_far, 0)

    neighbours = (strip > 0).astype(jnp.int32) + (strip < strips - 1).astype(jnp.int32)
    pl.semaphore_wait(barrier, 14 + neighbours)

    def t_copy(cls, dist):
        return pltpu.make_async_remote_copy(
            tsel.at[cls * 8 + dist], trecv.at[cls, dist],
            t_s.at[cls, dist - 1], t_r.at[cls, dist - 1],
            device_id=along(cls, dist), device_id_type=MESH,
        )

    def a_copy(cls, dist, k):
        return pltpu.make_async_remote_copy(
            abuf_s.at[cls, dist - 1, k], abuf_r.at[cls, dist, k],
            a_s.at[cls, dist - 1, k], a_r.at[cls, dist - 1, k],
            device_id=along(cls, dist), device_id_type=MESH,
        )

    for dist in ORDER:
        for cls in range(2):
            t_copy(cls, dist).start()

    def a_start(k, carry):
        for dist in ORDER:
            for cls in range(2):
                a_copy(cls, dist, k).start()
        return carry

    lax.fori_loop(0, 2, a_start, 0)

    for cls in range(2):
        pack(abuf_r.at[cls, 0], cls, 0)
        trecv[cls, 0] = tsel[cls * 8]

    idx = jnp.concatenate(
        [hsend_idx[...], hrecv_idx[...], jnp.zeros((4, 128), jnp.int32)], axis=0
    ).astype(F32)
    idx_t = idx.T
    hrows[...] = jnp.zeros_like(hrows)

    def gather(kc, carry):
        block = cols[pl.ds(kc * 4, 4)].reshape(256, 128)
        lane = lax.broadcasted_iota(jnp.int32, (128, 256), 1) + kc * 256
        lane = lane.astype(F32)
        for l in range(4):
            hot = jnp.where(idx_t[:, l : l + 1] == lane, 1.0, 0.0).astype(BF)
            hrows[l] += jnp.dot(hot, block, preferred_element_type=F32)
        return carry

    lax.fori_loop(0, 12, gather, 0)
    hsend[...] = hrows[pl.ds(0, 2)].astype(BF)

    def h_copy(way):
        step = 1 - 2 * way
        return pltpu.make_async_remote_copy(
            hsend.at[way], hrecv.at[way], h_s.at[way], h_r.at[way],
            device_id=(strip + step, dom), device_id_type=MESH,
        )

    @pl.when(strip < strips - 1)
    def _():
        h_copy(0).start()

    @pl.when(strip > 0)
    def _():
        h_copy(1).start()

    par = jnp.where(lax.broadcasted_iota(jnp.int32, (1, 128), 1) >= 64, 1.0, 0.0)
    twice = 2.0 * lax.broadcasted_iota(jnp.int32, (8, 128), 0).astype(F32)
    den[...] = jnp.zeros_like(den)

    def expand(cls, o, d, k):
        for rr in range(2):
            w = abuf_r[cls, d, k, pl.ds(128 + rr * 64, 64), :]
            u = tf[cls, d, pl.ds(2 * k + rr, 1), :] - par
            v = tr[cls, d, pl.ds(2 * k + rr, 1), :] - par
            wf = w.astype(F32)
            wrf = pltpu.roll(wf, 64, 1)
            wr = wrf.astype(BF)
            total = jnp.sum(wf, axis=0, keepdims=True)
            turned = jnp.sum(wrf, axis=0, keepdims=True)
            den[o] += jnp.where(u == twice, total, 0.0) + jnp.where(v == twice, turned, 0.0)
            ub = jnp.broadcast_to(u, (16, 128))
            vb = jnp.broadcast_to(v, (16, 128))
            rows = pl.ds(pl.multiple_of(d * 128 + rr * 64, 64), 64)
            for m in range(8):
                a = jnp.where(ub == 2.0 * m, 1.0, 0.0).astype(BF)
                b = jnp.where(vb == 2.0 * m, 1.0, 0.0).astype(BF)
                a4 = jnp.concatenate([a] * 4, axis=0)
                b4 = jnp.concatenate([b] * 4, axis=0)
                wexp[o, rows, pl.ds(m * 128, 128)] = w * a4 + wr * b4

    hcoord = (1 - q) * z + q * y
    ccoord = (1 - q) * y + q * z

    def tile_at(home, t):
        coord = hcoord if home else ccoord
        return (q if home else 1 - q) * 4 + lax.rem(coord + t + SIDE, SIDE) // 2

    def next_to(home, way):
        return along(1 - q if home else q, 1 - 2 * way)

    def add_up(t):
        home = t % 2 == 0
        k = 3 - t if t < 4 else t - 4
        cls = q if home else 1 - q
        o = tile_at(home, t)

        def source(e, carry):
            far = jnp.where(lax.rem(e, 2) == 0, 4 - e // 2, 4 + e // 2)
            d = jnp.where(e == 0, 0, far)

            @pl.when(e > 0)
            def _():
                a_copy(cls, jnp.maximum(d, 1), k).wait_recv()

            expand(cls, o, d, k)
            lanes = pl.ds(pl.multiple_of(d * 128, 128), 128)
            xt[:, lanes] = abuf_r[cls, d, k, pl.ds(0, 128), :].T
            return carry

        lax.fori_loop(0, 8, source, 0)
        for mm in range(4):
            part = jnp.dot(xt[...], wexp[o, :, pl.ds(mm * 256, 256)], preferred_element_type=F32)
            for h in range(2):
                acc[o, 2 * mm + h] = part[:, h * 128 : h * 128 + 128]

    def see(e, carry):
        cls, d = e // 8, lax.rem(e, 8)

        @pl.when(d > 0)
        def _():
            t_copy(cls, jnp.maximum(d, 1)).wait_recv()

        t = trecv[cls, d].astype(F32)[0:8]
        tf[cls, d] = t
        tr[cls, d] = pltpu.roll(t, 64, 1)
        return carry

    lax.fori_loop(0, 16, see, 0)

    def whole(t, way):
        half = CHUNKS // 2
        return (0, CHUNKS) if t < 4 else ((0, half), (half, CHUNKS))[way]

    def b_copy(t, way, ck):
        return pltpu.make_async_remote_copy(
            bsend.at[t - 1, way, ck], brecv.at[t - 1, way, ck],
            b_s.at[t - 1, way, ck], b_r.at[t - 1, way, ck],
            device_id=next_to(t % 2 == 0, way), device_id_type=MESH,
        )

    def b_total(t, way, ck, o):
        num = acc[o, ck]
        dd = den[o]
        if t < 4:
            wide = brecv[t, way, ck].astype(F32)
            num = num + wide[0:128]
            dd = dd + wide[128:136] + wide[136:144]
        return num, dd

    def b_hop(t, ways):
        def send(ck, way):
            o = tile_at(t % 2 == 0, t * (1 - 2 * way))
            if t == 4:
                ship(t, way, ck, *b_total(4, way, ck, o))
            elif t == 3:
                lo, hi = whole(4, way)
                further = (ck >= lo) & (ck < hi)

                @pl.when(further)
                def _():
                    b_copy(4, way, ck).wait_recv()
                    ship(t, way, ck, *b_total(t, way, ck, o))

                @pl.when(jnp.logical_not(further))
                def _():
                    ship(t, way, ck, *b_total(4, way, ck, o))
            else:
                b_copy(t + 1, way, ck).wait_recv()
                ship(t, way, ck, *b_total(t, way, ck, o))

        def both(ck, carry):
            for way in ways:
                send(ck, way)
            return carry

        if t == 4:
            half = CHUNKS // 2

            def four(ck, carry):
                send(ck, 0)
                send(ck + half, 1)
                return carry

            lax.fori_loop(0, half, four, 0)
        else:
            lax.fori_loop(0, CHUNKS, both, 0)

    def ship(t, way, ck, num, dd):
        high = dd.astype(BF)
        low = (dd - high.astype(F32)).astype(BF)
        bsend[t - 1, way, ck, pl.ds(0, 128), :] = num.astype(BF)
        bsend[t - 1, way, ck, pl.ds(128, 16), :] = jnp.concatenate([high, low], axis=0)
        b_copy(t, way, ck).start()

    add_up(4)
    b_hop(4, (0, 1))
    a_start(2, 0)
    add_up(3)
    add_up(5)
    b_hop(3, (0, 1))
    a_start(3, 0)

    @pl.when(strip > 0)
    def _():
        h_copy(0).wait_recv()

    @pl.when(strip == 0)
    def _():
        hrecv[0] = jnp.zeros((128, 128), BF)

    @pl.when(strip < strips - 1)
    def _():
        h_copy(1).wait_recv()

    @pl.when(strip == strips - 1)
    def _():
        hrecv[1] = jnp.zeros((128, 128), BF)

    keep = (
        jnp.where(strip > 0, 0.5, 0.0).astype(F32),
        jnp.where(strip < strips - 1, 0.5, 0.0).astype(F32),
    )
    for way in range(2):
        delta = keep[way] * (hrecv[way].astype(F32) - hrows[2 + way])
        high = delta.astype(BF)
        hrows[2 + way] = delta
        hsplit = (high, (delta - high.astype(F32)).astype(BF))
        if way == 0:
            split0 = hsplit
        else:
            split1 = hsplit
    highs = jnp.concatenate([split0[0], split1[0]], axis=0)
    lows = jnp.concatenate([split0[1], split1[1]], axis=0)

    def relax(kc, carry):
        row = (lax.broadcasted_iota(jnp.int32, (256, 128), 0) + kc * 256)
        hot = jnp.concatenate(
            [
                jnp.where(row == hrecv_idx[pl.ds(0, 1), :], 1.0, 0.0).astype(BF),
                jnp.where(row == hrecv_idx[pl.ds(1, 1), :], 1.0, 0.0).astype(BF),
            ],
            axis=1,
        )
        moved = jnp.dot(hot, highs, preferred_element_type=F32)
        moved += jnp.dot(hot, lows, preferred_element_type=F32)
        block = cols[pl.ds(kc * 4, 4)].reshape(256, 128).astype(F32)
        relaxed[pl.ds(kc * 4, 4)] = (block + moved).reshape(4, 64, 128)
        return carry

    lax.fori_loop(0, 12, relax, 0)

    add_up(2)
    add_up(6)
    b_hop(2, (0, 1))
    add_up(1)
    add_up(7)
    b_hop(1, (0, 1))
    own = tile_at(True, 0)
    add_up(0)

    def c_copy(t, way, ck):
        o = tile_at(t % 2 == 1, -(t - 1) * (1 - 2 * way))
        rows = pl.ds(pl.multiple_of(ck * 128, 128), 128)
        return pltpu.make_async_remote_copy(
            flux.at[o, rows], flux.at[o, rows], c_s.at[t - 1, way, ck], c_r.at[o, ck],
            device_id=next_to(t % 2 == 1, way), device_id_type=MESH,
        )

    def c_arrive(o, ck):
        rows = pl.ds(pl.multiple_of(ck * 128, 128), 128)
        pltpu.make_async_remote_copy(
            flux.at[o, rows], flux.at[o, rows], c_s.at[0, 0, 0], c_r.at[o, ck],
            device_id=next_to(True, 0), device_id_type=MESH,
        ).wait_recv()

    def finish(ck, carry):
        for way in range(2):
            b_copy(1, way, ck).wait_recv()
        wide = brecv[0, 0, ck].astype(F32) + brecv[0, 1, ck].astype(F32)
        dtot[...] = jnp.maximum(den[own] + wide[128:136] + wide[136:144], 1.0)
        rows = pl.ds(pl.multiple_of(ck * 128, 128), 128)
        g = ((acc[own, ck] + wide[0:128]) / dtot[pl.ds(ck, 1), :]).T.astype(BF)
        grid_out[rows, :] = g
        mixed = jnp.dot(g, coag[...], preferred_element_type=F32)
        flux[own, rows, :] = (gain[...] * jnp.tanh(mixed)).astype(BF)
        for way in range(2):
            c_copy(1, way, ck).start()
        return carry

    lax.fori_loop(0, CHUNKS, finish, 0)

    def d_copy(cls, k, dist):
        pair = pl.ds(k * 2, 2)
        o = cls * 4 + k
        return pltpu.make_async_remote_copy(
            dsend.at[cls, dist - 1, pair], drecv.at[pl.ds(cls * 64 + dist * 8 + k * 2, 2)],
            d_s.at[o, dist - 1], d_r.at[o, dist - 1],
            device_id=along(cls, SIDE - dist), device_id_type=MESH,
        )

    def back(o, k):
        cls = o // 4
        tile = flux[o]
        for pos in range(4):
            r = jnp.dot(
                wexp[o, pl.ds(pos * 256, 256), :], tile, preferred_element_type=F32
            ).astype(BF)
            for h in range(2):
                d = pos * 2 + h
                two = r[h * 128 : h * 128 + 128].reshape(2, 64, 128)
                if d == 0:
                    drecv[pl.ds(cls * 64 + k * 2, 2)] = two
                else:
                    dsend[cls, d - 1, pl.ds(k * 2, 2)] = two
        for dist in ORDER:
            d_copy(cls, k, dist).start()

    waiting = [(own, 3)]
    for t in (1, 2, 3):
        tiles = [tile_at(t % 2 == 0, -t * (1 - 2 * way)) for way in range(2)]

        def relay(ck, carry, t=t, tiles=tiles):
            for way in range(2):
                c_arrive(tiles[way], ck)
                lo, hi = whole(t + 1, way)

                @pl.when((ck >= lo) & (ck < hi))
                def _():
                    c_copy(t + 1, way, ck).start()

            return carry

        lax.fori_loop(0, CHUNKS, relay, 0)
        for pair in waiting:
            back(*pair)
        waiting = [(tiles[way], 4 - t - way) for way in range(2)]
    for pair in waiting:
        back(*pair)
    far = tile_at(True, 4)
    for ck in range(CHUNKS):
        c_arrive(far, ck)
    back(far, 0)

    def a_sent(k, carry):
        for dist in range(1, SIDE):
            for cls in range(2):
                a_copy(cls, dist, k).wait_send()
        return carry

    lax.fori_loop(0, PARTS, a_sent, 0)
    for dist in range(1, SIDE):
        for cls in range(2):
            t_copy(cls, dist).wait_send()

    @pl.when(strip < strips - 1)
    def _():
        h_copy(0).wait_send()

    @pl.when(strip > 0)
    def _():
        h_copy(1).wait_send()

    for t in range(1, 5):
        for way in range(2):
            for ck in range(*whole(t, way)):
                b_copy(t, way, ck).wait_send()
                c_copy(t, way, ck).wait_send()

    def gather_back(o, carry):
        for dist in range(1, SIDE):
            d_copy(o // 4, lax.rem(o, 4), dist).wait_recv()
        return carry

    lax.fori_loop(0, 8, gather_back, 0)

    def final(j, carry):
        cols_out[j] = (relaxed[j] + drecv[slot_of[j]].astype(F32)).astype(BF)
        return carry

    lax.fori_loop(0, 48, final, 0)

    def d_sent(o, carry):
        for dist in range(1, SIDE):
            d_copy(o // 4, lax.rem(o, 4), dist).wait_send()
        return carry

    lax.fori_loop(0, 8, d_sent, 0)


def shards(
    columns, regrid_weights, owner_table, grid_targets, halo_send, halo_recv, coag, settle_gain
):
    nblocks, blk, chans = regrid_weights.shape[1], regrid_weights.shape[2], columns.shape[2]
    dom = lax.axis_index("dom")
    y, z = dom // SIDE, lax.rem(dom, SIDE)
    owners = owner_table[0, :, 0]
    ids = jnp.arange(nblocks, dtype=jnp.int32)
    rank = jnp.sum(
        ((owners[:, None] == owners[None, :]) & (ids[None, :] < ids[:, None])).astype(jnp.int32),
        axis=1,
    )
    oy, oz = owners // SIDE, lax.rem(owners, SIDE)
    cls = lax.rem(oy + oz, 2)
    dist = jnp.where(cls == 0, oy - y + SIDE, oz - z + SIDE) % SIDE
    away = jnp.where(cls == 0, oz - z + SIDE, oy - y + SIDE) % SIDE
    slot_of = cls * 64 + dist * 8 + jnp.where(away < 4, 3 - away, away - 4) * 2 + rank
    hot = slot_of[None, :] == jnp.arange(128, dtype=jnp.int32)[:, None]
    tab = jnp.max(jnp.where(hot, ids[None, :], 0), axis=1)
    t01 = jnp.max(jnp.where(hot[:, None, :], grid_targets[0].T[None], -1), axis=2)
    tsel = jnp.repeat(t01, 64, axis=1).astype(BF).reshape(16, 8, 128)
    tsel = jnp.concatenate([tsel, tsel], axis=1)

    vmem = pl.BlockSpec(memory_space=pltpu.VMEM)
    smem = pl.BlockSpec(memory_space=pltpu.SMEM)
    dma = pltpu.SemaphoreType.DMA
    grid, out = pl.pallas_call(
        kernel,
        out_shape=(
            jax.ShapeDtypeStruct((1024, chans), BF),
            jax.ShapeDtypeStruct((nblocks, blk, chans), BF),
        ),
        in_specs=[smem, smem] + [vmem] * 7,
        out_specs=(vmem, vmem),
        scratch_shapes=[
            pltpu.VMEM((2, 7, PARTS, 256, 128), BF),
            pltpu.VMEM((2, 8, PARTS, 256, 128), BF),
            pltpu.VMEM((2, 8, 16, 128), BF),
            pltpu.VMEM((2, 8, 8, 128), F32),
            pltpu.VMEM((2, 8, 8, 128), F32),
            pltpu.VMEM((128, 1024), BF),
            pltpu.VMEM((8, 1024, 1024), BF),
            pltpu.VMEM((8, 8, 128, 128), F32),
            pltpu.VMEM((8, 8, 128), F32),
            pltpu.VMEM((4, 2, CHUNKS, 144, 128), BF),
            pltpu.VMEM((4, 2, CHUNKS, 144, 128), BF),
            pltpu.VMEM((8, 128), F32),
            pltpu.VMEM((8, 1024, 128), BF),
            pltpu.VMEM((2, 7, 8, 64, 128), BF),
            pltpu.VMEM((128, 64, 128), BF),
            pltpu.VMEM((48, 64, 128), F32),
            pltpu.VMEM((4, 128, 128), F32),
            pltpu.VMEM((2, 128, 128), BF),
            pltpu.VMEM((2, 128, 128), BF),
            dma((2, 7)), dma((2, 7)),
            dma((2, 7, PARTS)), dma((2, 7, PARTS)),
            dma((4, 2, CHUNKS)), dma((4, 2, CHUNKS)),
            dma((4, 2, CHUNKS)), dma((8, CHUNKS)),
            dma((8, 7)), dma((8, 7)),
            dma((2,)), dma((2,)),
        ],
        compiler_params=pltpu.CompilerParams(
            collective_id=0, has_side_effects=True, vmem_limit_bytes=56 * 2**20
        ),
    )(
        tab, slot_of, tsel,
        columns[0].reshape(nblocks, blk, chans), regrid_weights[0],
        halo_send[0, 0], halo_recv[0, 0], coag, settle_gain[None, :],
    )
    return grid[None], out.reshape(1, nblocks * blk, chans)


def solution(mesh):
    placed = (
        P("strip", "dom", None),
        P("strip", "dom", None, None),
        P("strip", "dom", None),
        P("strip", "dom", None),
        P("strip", "dom", None, None),
        P("strip", "dom", None, None),
        P(),
        P(),
    )
    return jax.shard_map(
        shards,
        mesh=mesh,
        in_specs=placed,
        out_specs=(P("strip", "dom", None), P("strip", "dom", None)),
        check_vma=False,
    )
```

```python
import jax
import jax.numpy as jnp
from jax import lax
from jax.experimental import pallas as pl
from jax.experimental.pallas import tpu as pltpu
from jax.sharding import PartitionSpec as P

MESH = pl.DeviceIdType.MESH
BF = jnp.bfloat16
F32 = jnp.float32
SIDE = 8
CHUNKS = 8
ORDER = (4, 3, 5, 2, 6, 1, 7)
PARTS = 4


def kernel(
    tab, slot_of, tsel, cols, wts, hsend_idx, hrecv_idx, coag, gain,
    grid_out, cols_out,
    abuf_s, abuf_r, trecv, tf, tr, xt, wexp, acc, den, bsend, brecv, dtot, flux, dsend, drecv,
    relaxed, hrows, hsend, hrecv,
    t_s, t_r, a_s, a_r, b_s, b_r, c_s, c_r, d_s, d_r, h_s, h_r,
):
    strip = lax.axis_index("strip")
    dom = lax.axis_index("dom")
    strips = lax.axis_size("strip")
    y = dom // SIDE
    z = lax.rem(dom, SIDE)
    q = lax.rem(y + z, 2)

    def along(cls, dist):
        ny = lax.rem(y + (1 - cls) * dist + SIDE, SIDE)
        nz = lax.rem(z + cls * dist + SIDE, SIDE)
        return (strip, ny * SIDE + nz)

    barrier = pltpu.get_barrier_semaphore()
    for cls in range(2):
        for dist in range(1, SIDE):
            pl.semaphore_signal(barrier, inc=1, device_id=along(cls, dist), device_id_type=MESH)

    @pl.when(strip > 0)
    def _():
        pl.semaphore_signal(barrier, inc=1, device_id=(strip - 1, dom), device_id_type=MESH)

    @pl.when(strip < strips - 1)
    def _():
        pl.semaphore_signal(barrier, inc=1, device_id=(strip + 1, dom), device_id_type=MESH)

    def pack(dst, cls, dist):
        base = cls * 64 + dist * 8

        def one(k, carry):
            for r in range(2):
                j = tab[base + k * 2 + r]
                dst[k, pl.ds(r * 64, 64), :] = cols[j]
                dst[k, pl.ds(128 + r * 64, 64), :] = wts[j]
            return carry

        lax.fori_loop(0, PARTS, one, 0)

    def pack_far(t, carry):
        cls, dist = t // 7, lax.rem(t, 7) + 1
        pack(abuf_s.at[cls, dist - 1], cls, dist)
        return carry

    lax.fori_loop(0, 14, pack_far, 0)

    neighbours = (strip > 0).astype(jnp.int32) + (strip < strips - 1).astype(jnp.int32)
    pl.semaphore_wait(barrier, 14 + neighbours)

    def t_copy(cls, dist):
        return pltpu.make_async_remote_copy(
            tsel.at[cls * 8 + dist], trecv.at[cls, dist],
            t_s.at[cls, dist - 1], t_r.at[cls, dist - 1],
            device_id=along(cls, dist), device_id_type=MESH,
        )

    def a_copy(cls, dist, k):
        return pltpu.make_async_remote_copy(
            abuf_s.at[cls, dist - 1, k], abuf_r.at[cls, dist, k],
            a_s.at[cls, dist - 1, k], a_r.at[cls, dist - 1, k],
            device_id=along(cls, dist), device_id_type=MESH,
        )

    for dist in ORDER:
        for cls in range(2):
            t_copy(cls, dist).start()

    def a_start(k, carry):
        for dist in ORDER:
            for cls in range(2):
                a_copy(cls, dist, k).start()
        return carry

    lax.fori_loop(0, 2, a_start, 0)

    for cls in range(2):
        pack(abuf_r.at[cls, 0], cls, 0)
        trecv[cls, 0] = tsel[cls * 8]

    idx = jnp.concatenate(
        [hsend_idx[...], hrecv_idx[...], jnp.zeros((4, 128), jnp.int32)], axis=0
    ).astype(F32)
    idx_t = idx.T
    hrows[...] = jnp.zeros_like(hrows)

    def gather(kc, carry):
        block = cols[pl.ds(kc * 4, 4)].reshape(256, 128)
        lane = lax.broadcasted_iota(jnp.int32, (128, 256), 1) + kc * 256
        lane = lane.astype(F32)
        for l in range(4):
            hot = jnp.where(idx_t[:, l : l + 1] == lane, 1.0, 0.0).astype(BF)
            hrows[l] += jnp.dot(hot, block, preferred_element_type=F32)
        return carry

    lax.fori_loop(0, 12, gather, 0)
    hsend[...] = hrows[pl.ds(0, 2)].astype(BF)

    def h_copy(way):
        step = 1 - 2 * way
        return pltpu.make_async_remote_copy(
            hsend.at[way], hrecv.at[way], h_s.at[way], h_r.at[way],
            device_id=(strip + step, dom), device_id_type=MESH,
        )

    @pl.when(strip < strips - 1)
    def _():
        h_copy(0).start()

    @pl.when(strip > 0)
    def _():
        h_copy(1).start()

    par = jnp.where(lax.broadcasted_iota(jnp.int32, (1, 128), 1) >= 64, 1.0, 0.0)
    twice = 2.0 * lax.broadcasted_iota(jnp.int32, (8, 128), 0).astype(F32)
    den[...] = jnp.zeros_like(den)

    def expand(cls, o, d, k):
        for rr in range(2):
            w = abuf_r[cls, d, k, pl.ds(128 + rr * 64, 64), :]
            u = tf[cls, d, pl.ds(2 * k + rr, 1), :] - par
            v = tr[cls, d, pl.ds(2 * k + rr, 1), :] - par
            wf = w.astype(F32)
            wrf = pltpu.roll(wf, 64, 1)
            wr = wrf.astype(BF)
            total = jnp.sum(wf, axis=0, keepdims=True)
            turned = jnp.sum(wrf, axis=0, keepdims=True)
            den[o] += jnp.where(u == twice, total, 0.0) + jnp.where(v == twice, turned, 0.0)
            ub = jnp.broadcast_to(u, (16, 128))
            vb = jnp.broadcast_to(v, (16, 128))
            rows = pl.ds(pl.multiple_of(d * 128 + rr * 64, 64), 64)
            for m in range(8):
                a = jnp.where(ub == 2.0 * m, 1.0, 0.0).astype(BF)
                b = jnp.where(vb == 2.0 * m, 1.0, 0.0).astype(BF)
                a4 = jnp.concatenate([a] * 4, axis=0)
                b4 = jnp.concatenate([b] * 4, axis=0)
                wexp[o, rows, pl.ds(m * 128, 128)] = w * a4 + wr * b4

    hcoord = (1 - q) * z + q * y
    ccoord = (1 - q) * y + q * z

    def tile_at(home, t):
        coord = hcoord if home else ccoord
        return (q if home else 1 - q) * 4 + lax.rem(coord + t + SIDE, SIDE) // 2

    def next_to(home, way):
        return along(1 - q if home else q, 1 - 2 * way)

    def add_up(t):
        home = t % 2 == 0
        k = 3 - t if t < 4 else t - 4
        cls = q if home else 1 - q
        o = tile_at(home, t)

        def source(e, carry):
            far = jnp.where(lax.rem(e, 2) == 0, 4 - e // 2, 4 + e // 2)
            d = jnp.where(e == 0, 0, far)

            @pl.when(e > 0)
            def _():
                a_copy(cls, jnp.maximum(d, 1), k).wait_recv()

            expand(cls, o, d, k)
            lanes = pl.ds(pl.multiple_of(d * 128, 128), 128)
            xt[:, lanes] = abuf_r[cls, d, k, pl.ds(0, 128), :].T
            return carry

        lax.fori_loop(0, 8, source, 0)
        for mm in range(4):
            part = jnp.dot(xt[...], wexp[o, :, pl.ds(mm * 256, 256)], preferred_element_type=F32)
            for h in range(2):
                acc[o, 2 * mm + h] = part[:, h * 128 : h * 128 + 128]

    def see(e, carry):
        cls, d = e // 8, lax.rem(e, 8)

        @pl.when(d > 0)
        def _():
            t_copy(cls, jnp.maximum(d, 1)).wait_recv()

        t = trecv[cls, d].astype(F32)[0:8]
        tf[cls, d] = t
        tr[cls, d] = pltpu.roll(t, 64, 1)
        return carry

    lax.fori_loop(0, 16, see, 0)

    def whole(t, way):
        half = CHUNKS // 2
        return (0, CHUNKS) if t < 4 else ((0, half), (half, CHUNKS))[way]

    def b_copy(t, way, ck):
        return pltpu.make_async_remote_copy(
            bsend.at[t - 1, way, ck], brecv.at[t - 1, way, ck],
            b_s.at[t - 1, way, ck], b_r.at[t - 1, way, ck],
            device_id=next_to(t % 2 == 0, way), device_id_type=MESH,
        )

    def b_total(t, way, ck, o):
        num = acc[o, ck]
        dd = den[o]
        if t < 4:
            wide = brecv[t, way, ck].astype(F32)
            num = num + wide[0:128]
            dd = dd + wide[128:136] + wide[136:144]
        return num, dd

    def b_hop(t, ways):
        def send(ck, way):
            o = tile_at(t % 2 == 0, t * (1 - 2 * way))
            if t == 4:
                ship(t, way, ck, *b_total(4, way, ck, o))
            elif t == 3:
                lo, hi = whole(4, way)
                further = (ck >= lo) & (ck < hi)

                @pl.when(further)
                def _():
                    b_copy(4, way, ck).wait_recv()
                    ship(t, way, ck, *b_total(t, way, ck, o))

                @pl.when(jnp.logical_not(further))
                def _():
                    ship(t, way, ck, *b_total(4, way, ck, o))
            else:
                b_copy(t + 1, way, ck).wait_recv()
                ship(t, way, ck, *b_total(t, way, ck, o))

        def both(ck, carry):
            for way in ways:
                send(ck, way)
            return carry

        if t == 4:
            half = CHUNKS // 2

            def four(ck, carry):
                send(ck, 0)
                send(ck + half, 1)
                return carry

            lax.fori_loop(0, half, four, 0)
        else:
            lax.fori_loop(0, CHUNKS, both, 0)

    def ship(t, way, ck, num, dd):
        high = dd.astype(BF)
        low = (dd - high.astype(F32)).astype(BF)
        bsend[t - 1, way, ck, pl.ds(0, 128), :] = num.astype(BF)
        bsend[t - 1, way, ck, pl.ds(128, 16), :] = jnp.concatenate([high, low], axis=0)
        b_copy(t, way, ck).start()

    add_up(4)
    b_hop(4, (0, 1))
    a_start(2, 0)
    add_up(3)
    add_up(5)
    b_hop(3, (0, 1))
    a_start(3, 0)

    @pl.when(strip > 0)
    def _():
        h_copy(0).wait_recv()

    @pl.when(strip == 0)
    def _():
        hrecv[0] = jnp.zeros((128, 128), BF)

    @pl.when(strip < strips - 1)
    def _():
        h_copy(1).wait_recv()

    @pl.when(strip == strips - 1)
    def _():
        hrecv[1] = jnp.zeros((128, 128), BF)

    keep = (
        jnp.where(strip > 0, 0.5, 0.0).astype(F32),
        jnp.where(strip < strips - 1, 0.5, 0.0).astype(F32),
    )
    for way in range(2):
        delta = keep[way] * (hrecv[way].astype(F32) - hrows[2 + way])
        high = delta.astype(BF)
        hrows[2 + way] = delta
        hsplit = (high, (delta - high.astype(F32)).astype(BF))
        if way == 0:
            split0 = hsplit
        else:
            split1 = hsplit
    highs = jnp.concatenate([split0[0], split1[0]], axis=0)
    lows = jnp.concatenate([split0[1], split1[1]], axis=0)

    def relax(kc, carry):
        row = (lax.broadcasted_iota(jnp.int32, (256, 128), 0) + kc * 256)
        hot = jnp.concatenate(
            [
                jnp.where(row == hrecv_idx[pl.ds(0, 1), :], 1.0, 0.0).astype(BF),
                jnp.where(row == hrecv_idx[pl.ds(1, 1), :], 1.0, 0.0).astype(BF),
            ],
            axis=1,
        )
        moved = jnp.dot(hot, highs, preferred_element_type=F32)
        moved += jnp.dot(hot, lows, preferred_element_type=F32)
        block = cols[pl.ds(kc * 4, 4)].reshape(256, 128).astype(F32)
        relaxed[pl.ds(kc * 4, 4)] = (block + moved).reshape(4, 64, 128)
        return carry

    lax.fori_loop(0, 12, relax, 0)

    add_up(2)
    add_up(6)
    b_hop(2, (0, 1))
    add_up(1)
    add_up(7)
    b_hop(1, (0, 1))
    own = tile_at(True, 0)
    add_up(0)

    def c_copy(t, way, ck):
        o = tile_at(t % 2 == 1, -(t - 1) * (1 - 2 * way))
        rows = pl.ds(pl.multiple_of(ck * 128, 128), 128)
        return pltpu.make_async_remote_copy(
            flux.at[o, rows], flux.at[o, rows], c_s.at[t - 1, way, ck], c_r.at[o, ck],
            device_id=next_to(t % 2 == 1, way), device_id_type=MESH,
        )

    def c_arrive(o, ck):
        rows = pl.ds(pl.multiple_of(ck * 128, 128), 128)
        pltpu.make_async_remote_copy(
            flux.at[o, rows], flux.at[o, rows], c_s.at[0, 0, 0], c_r.at[o, ck],
            device_id=next_to(True, 0), device_id_type=MESH,
        ).wait_recv()

    def finish(ck, carry):
        for way in range(2):
            b_copy(1, way, ck).wait_recv()
        wide = brecv[0, 0, ck].astype(F32) + brecv[0, 1, ck].astype(F32)
        dtot[...] = jnp.maximum(den[own] + wide[128:136] + wide[136:144], 1.0)
        rows = pl.ds(pl.multiple_of(ck * 128, 128), 128)
        g = ((acc[own, ck] + wide[0:128]) / dtot[pl.ds(ck, 1), :]).T.astype(BF)
        grid_out[rows, :] = g
        mixed = jnp.dot(g, coag[...], preferred_element_type=F32)
        flux[own, rows, :] = (gain[...] * jnp.tanh(mixed)).astype(BF)
        for way in range(2):
            c_copy(1, way, ck).start()
        return carry

    lax.fori_loop(0, CHUNKS, finish, 0)

    def d_copy(cls, k, dist):
        pair = pl.ds(k * 2, 2)
        o = cls * 4 + k
        return pltpu.make_async_remote_copy(
            dsend.at[cls, dist - 1, pair], drecv.at[pl.ds(cls * 64 + dist * 8 + k * 2, 2)],
            d_s.at[o, dist - 1], d_r.at[o, dist - 1],
            device_id=along(cls, SIDE - dist), device_id_type=MESH,
        )

    def back(o, k):
        cls = o // 4
        tile = flux[o]
        for pos in range(4):
            r = jnp.dot(
                wexp[o, pl.ds(pos * 256, 256), :], tile, preferred_element_type=F32
            ).astype(BF)
            for h in range(2):
                d = pos * 2 + h
                two = r[h * 128 : h * 128 + 128].reshape(2, 64, 128)
                if d == 0:
                    drecv[pl.ds(cls * 64 + k * 2, 2)] = two
                else:
                    dsend[cls, d - 1, pl.ds(k * 2, 2)] = two
        for dist in ORDER:
            d_copy(cls, k, dist).start()

    waiting = [(own, 3)]
    for t in (1, 2, 3):
        tiles = [tile_at(t % 2 == 0, -t * (1 - 2 * way)) for way in range(2)]

        def relay(ck, carry, t=t, tiles=tiles):
            for way in range(2):
                c_arrive(tiles[way], ck)
                lo, hi = whole(t + 1, way)

                @pl.when((ck >= lo) & (ck < hi))
                def _():
                    c_copy(t + 1, way, ck).start()

            return carry

        lax.fori_loop(0, CHUNKS, relay, 0)
        if t != 2:
            for pair in waiting:
                back(*pair)
            waiting = []
        waiting = waiting + [(tiles[way], 4 - t - way) for way in range(2)]
    for pair in waiting:
        back(*pair)
    far = tile_at(True, 4)
    for ck in range(CHUNKS):
        c_arrive(far, ck)
    back(far, 0)

    def a_sent(k, carry):
        for dist in range(1, SIDE):
            for cls in range(2):
                a_copy(cls, dist, k).wait_send()
        return carry

    lax.fori_loop(0, PARTS, a_sent, 0)
    for dist in range(1, SIDE):
        for cls in range(2):
            t_copy(cls, dist).wait_send()

    @pl.when(strip < strips - 1)
    def _():
        h_copy(0).wait_send()

    @pl.when(strip > 0)
    def _():
        h_copy(1).wait_send()

    for t in range(1, 5):
        for way in range(2):
            for ck in range(*whole(t, way)):
                b_copy(t, way, ck).wait_send()
                c_copy(t, way, ck).wait_send()

    def gather_back(o, carry):
        for dist in range(1, SIDE):
            d_copy(o // 4, lax.rem(o, 4), dist).wait_recv()
        return carry

    lax.fori_loop(0, 8, gather_back, 0)

    def final(j, carry):
        cols_out[j] = (relaxed[j] + drecv[slot_of[j]].astype(F32)).astype(BF)
        return carry

    lax.fori_loop(0, 48, final, 0)

    def d_sent(o, carry):
        for dist in range(1, SIDE):
            d_copy(o // 4, lax.rem(o, 4), dist).wait_send()
        return carry

    lax.fori_loop(0, 8, d_sent, 0)


def shards(
    columns, regrid_weights, owner_table, grid_targets, halo_send, halo_recv, coag, settle_gain
):
    nblocks, blk, chans = regrid_weights.shape[1], regrid_weights.shape[2], columns.shape[2]
    dom = lax.axis_index("dom")
    y, z = dom // SIDE, lax.rem(dom, SIDE)
    owners = owner_table[0, :, 0]
    ids = jnp.arange(nblocks, dtype=jnp.int32)
    rank = jnp.sum(
        ((owners[:, None] == owners[None, :]) & (ids[None, :] < ids[:, None])).astype(jnp.int32),
        axis=1,
    )
    oy, oz = owners // SIDE, lax.rem(owners, SIDE)
    cls = lax.rem(oy + oz, 2)
    dist = jnp.where(cls == 0, oy - y + SIDE, oz - z + SIDE) % SIDE
    away = jnp.where(cls == 0, oz - z + SIDE, oy - y + SIDE) % SIDE
    slot_of = cls * 64 + dist * 8 + jnp.where(away < 4, 3 - away, away - 4) * 2 + rank
    hot = slot_of[None, :] == jnp.arange(128, dtype=jnp.int32)[:, None]
    tab = jnp.max(jnp.where(hot, ids[None, :], 0), axis=1)
    t01 = jnp.max(jnp.where(hot[:, None, :], grid_targets[0].T[None], -1), axis=2)
    tsel = jnp.repeat(t01, 64, axis=1).astype(BF).reshape(16, 8, 128)
    tsel = jnp.concatenate([tsel, tsel], axis=1)

    vmem = pl.BlockSpec(memory_space=pltpu.VMEM)
    smem = pl.BlockSpec(memory_space=pltpu.SMEM)
    dma = pltpu.SemaphoreType.DMA
    grid, out = pl.pallas_call(
        kernel,
        out_shape=(
            jax.ShapeDtypeStruct((1024, chans), BF),
            jax.ShapeDtypeStruct((nblocks, blk, chans), BF),
        ),
        in_specs=[smem, smem] + [vmem] * 7,
        out_specs=(vmem, vmem),
        scratch_shapes=[
            pltpu.VMEM((2, 7, PARTS, 256, 128), BF),
            pltpu.VMEM((2, 8, PARTS, 256, 128), BF),
            pltpu.VMEM((2, 8, 16, 128), BF),
            pltpu.VMEM((2, 8, 8, 128), F32),
            pltpu.VMEM((2, 8, 8, 128), F32),
            pltpu.VMEM((128, 1024), BF),
            pltpu.VMEM((8, 1024, 1024), BF),
            pltpu.VMEM((8, 8, 128, 128), F32),
            pltpu.VMEM((8, 8, 128), F32),
            pltpu.VMEM((4, 2, CHUNKS, 144, 128), BF),
            pltpu.VMEM((4, 2, CHUNKS, 144, 128), BF),
            pltpu.VMEM((8, 128), F32),
            pltpu.VMEM((8, 1024, 128), BF),
            pltpu.VMEM((2, 7, 8, 64, 128), BF),
            pltpu.VMEM((128, 64, 128), BF),
            pltpu.VMEM((48, 64, 128), F32),
            pltpu.VMEM((4, 128, 128), F32),
            pltpu.VMEM((2, 128, 128), BF),
            pltpu.VMEM((2, 128, 128), BF),
            dma((2, 7)), dma((2, 7)),
            dma((2, 7, PARTS)), dma((2, 7, PARTS)),
            dma((4, 2, CHUNKS)), dma((4, 2, CHUNKS)),
            dma((4, 2, CHUNKS)), dma((8, CHUNKS)),
            dma((8, 7)), dma((8, 7)),
            dma((2,)), dma((2,)),
        ],
        compiler_params=pltpu.CompilerParams(
            collective_id=0, has_side_effects=True, vmem_limit_bytes=56 * 2**20
        ),
    )(
        tab, slot_of, tsel,
        columns[0].reshape(nblocks, blk, chans), regrid_weights[0],
        halo_send[0, 0], halo_recv[0, 0], coag, settle_gain[None, :],
    )
    return grid[None], out.reshape(1, nblocks * blk, chans)


def solution(mesh):
    placed = (
        P("strip", "dom", None),
        P("strip", "dom", None, None),
        P("strip", "dom", None),
        P("strip", "dom", None),
        P("strip", "dom", None, None),
        P("strip", "dom", None, None),
        P(),
        P(),
    )
    return jax.shard_map(
        shards,
        mesh=mesh,
        in_specs=placed,
        out_specs=(P("strip", "dom", None), P("strip", "dom", None)),
        check_vma=False,
    )
```
